32 devices in a mesh: clip: 8 (over z, x), freq: 4 (over y, core).
Axes of the slice: x: 2, y: 2, z: 4, core: 2. Of those that a mesh axis runs over, the one named last changes fastest.
Arguments:
- tokens: bfloat16 [8, 1188, 768], P('clip', 'freq'), may hold values from -6 to 6
- grad_out: bfloat16 [8, 1188, 768], P('clip', 'freq'), may hold values from -6 to 6
- freq_keep: int32 [8, 12], P('clip'), may hold values from 0 to 1, as said below
- lengths: int32 [8], P('clip'), may hold values from 49 to 99
- first_gain: float32 [768], replicated, may hold values from 0.25 to 1.75
- first_shift: float32 [768], replicated, may hold values from -1.75 to 1.75
- qkv_weight: bfloat16 [768, 2304], replicated, may hold values from -0.21875 to 0.21875
- query_bias: float32 [768], replicated, may hold values from -1.75 to 1.75
- value_bias: float32 [768], replicated, may hold values from -0.1875 to 0.1875
- proj_weight: bfloat16 [768, 768], replicated, may hold values from -4 to 4
- proj_bias: float32 [768], replicated, may hold values from -1.75 to 1.75
- second_gain: float32 [768], replicated, may hold values from 0.25 to 1.75
- second_shift: float32 [768], replicated, may hold values from -1.75 to 1.75
- up_weight: bfloat16 [768, 3072], replicated, may hold values from -0.21875 to 0.21875
- up_bias: float32 [3072], replicated, may hold values from -1.75 to 1.75
- down_weight: bfloat16 [3072, 768], replicated, may hold values from -0.109375 to 0.109375
- down_bias: float32 [768], replicated, may hold values from -1.75 to 1.75
Outputs:
- block_out: bfloat16 [8, 1188, 768], P('clip', 'freq')
- grad_tokens: bfloat16 [8, 1188, 768], P('clip', 'freq')
- grad_first_gain: float32 [768], P(('clip', 'freq'))
- grad_first_shift: float32 [768], P(('clip', 'freq'))
- grad_qkv_weight: float32 [768, 2304], P(('clip', 'freq'))
- grad_query_bias: float32 [768], P(('clip', 'freq'))
- grad_value_bias: float32 [768], P(('clip', 'freq'))
- grad_proj_weight: float32 [768, 768], P(('clip', 'freq'))
- grad_proj_bias: float32 [768], P(('clip', 'freq'))
- grad_second_gain: float32 [768], P(('clip', 'freq'))
- grad_second_shift: float32 [768], P(('clip', 'freq'))
- grad_up_weight: float32 [768, 3072], P(('clip', 'freq'))
- grad_up_bias: float32 [3072], P(('clip', 'freq'))
- grad_down_weight: float32 [3072, 768], P(('clip', 'freq'))
- grad_down_bias: float32 [768], P(('clip', 'freq'))
The draws below stay inside these ranges and needn't reach their ends.
Inputs may be any that keep to these rules, and one draw needn't show every extreme that they name: `freq_keep`: every clip keeps at least one frequency row among those of each index of freq.
All inputs are finite; a program needn't handle non-finite values.
Results may differ from the reference program's by a relative error of at most 0.014.
Values may be sent and summed in bfloat16 or wider, within the bound.
A program may use at most 128 MiB of HBM per device.

```python
import jax
import jax.numpy as jnp
from jax import lax

D = 768
HEADS = 12
HEAD_DIM = 64
FF = 3072
FREQ_ROWS = 12
TIME_COLS = 99
SLOTS = 1188
CLIPS = 8
N_FREQ = 4


def whole_clips(key):
    coin_flags = jax.random.randint(key, (CLIPS,), 0, 2)
    chosen_clip = jax.random.randint(jax.random.fold_in(key, 11), (), 0, CLIPS)
    forced_one = (jnp.arange(CLIPS) == chosen_clip).astype(jnp.int32)
    return jnp.maximum(coin_flags, forced_one)


def draw_lengths(key, part):
    complete = whole_clips(key)
    key = jax.random.fold_in(key, 3)
    shorter = jax.random.randint(key, (CLIPS,), TIME_COLS // 2, TIME_COLS + 1)
    return jnp.where(complete > 0, TIME_COLS, shorter).astype(jnp.int32)


def draw_freq_keep(key, part):
    complete = whole_clips(key)
    key = jax.random.fold_in(key, 5)
    group_size = FREQ_ROWS // N_FREQ
    random_bits = jax.random.randint(key, (CLIPS, FREQ_ROWS), 0, 2)
    offsets = jax.random.randint(jax.random.fold_in(key, 1), (CLIPS, N_FREQ), 0, group_size)
    row_index = jnp.arange(FREQ_ROWS)
    forced = (offsets[:, row_index // group_size] == (row_index % group_size)[None, :]).astype(jnp.int32)
    return jnp.maximum(jnp.maximum(random_bits, forced), complete[:, None]).astype(jnp.int32)


def steps_of(own_key, dims, cuts, smallest, high):
    level, own = 1.0, jax.random.fold_in(own_key, 6)
    for axis_at, blocks in cuts:
        steps = jnp.exp(jax.random.uniform(jax.random.fold_in(own, axis_at), (blocks,), jnp.float32, smallest / len(cuts), high / len(cuts)))
        level = level * jnp.repeat(steps, dims[axis_at] // blocks).reshape([-1 if axis == axis_at else 1 for axis in range(len(dims))])
    return level


def bell_draw(stream_key, dims, width, bound, cuts=(), held_as=jnp.bfloat16):
    factor_of = steps_of(stream_key, dims, cuts, -0.22, 0.18) if cuts else 1.0
    entries = jax.random.normal(stream_key, dims, jnp.float32) * width * factor_of
    return jnp.minimum(jnp.maximum(entries, -bound), bound).astype(held_as)


def setup_inputs(seed: int = 0) -> dict:
    key_of = jax.random.split(jax.random.key(seed), 18)
    return {
        "tokens": bell_draw(key_of[0], (CLIPS, SLOTS, D), 1.0, 6.0, ((0, 8), (1, 4))),
        "grad_out": bell_draw(key_of[1], (CLIPS, SLOTS, D), 1.0, 6.0, ((0, 8), (1, 4))),
        "freq_keep": draw_freq_keep(jax.random.fold_in(key_of[17], 71), 0),
        "lengths": draw_lengths(jax.random.fold_in(key_of[17], 71), 0),
        "first_gain": jnp.clip(1.0 + 0.15 * jax.random.normal(key_of[4], (D,), jnp.float32), 0.25, 1.75),
        "first_shift": bell_draw(key_of[5], (D,), 0.3, 1.75, (), jnp.float32),
        "qkv_weight": bell_draw(key_of[6], (D, 3 * D), D ** -0.5, 0.21875),
        "query_bias": bell_draw(key_of[7], (D,), 0.3, 1.75, (), jnp.float32),
        "value_bias": bell_draw(key_of[8], (D,), 0.03, 0.1875, (), jnp.float32),
        "proj_weight": bell_draw(key_of[9], (D, D), (max(4 * D // SLOTS, 1)) ** -0.5, 4.0),
        "proj_bias": bell_draw(key_of[10], (D,), 0.3, 1.75, (), jnp.float32),
        "second_gain": jnp.clip(1.0 + 0.15 * jax.random.normal(key_of[11], (D,), jnp.float32), 0.25, 1.75),
        "second_shift": bell_draw(key_of[12], (D,), 0.3, 1.75, (), jnp.float32),
        "up_weight": bell_draw(key_of[13], (D, FF), D ** -0.5, 0.21875),
        "up_bias": bell_draw(key_of[14], (FF,), 0.3, 1.75, (), jnp.float32),
        "down_weight": bell_draw(key_of[15], (FF, D), FF ** -0.5, 0.109375),
        "down_bias": bell_draw(key_of[16], (D,), 0.3, 1.75, (), jnp.float32),
    }


EPS = 1e-06

@jax.custom_vjp
def low(v):
    return lax.optimization_barrier(v.astype(jnp.bfloat16)).astype(jnp.float32)

@jax.custom_vjp
def low_back(v):
    return v

def low_keep(v):
    return (low(v), None)

def low_pass(kept, grad):
    return (grad,)

def back_keep(v):
    return (v, None)

def back_low(kept, grad):
    return (low(grad),)
low.defvjp(low_keep, low_pass)
low_back.defvjp(back_keep, back_low)

def layer_norm(values, gain, shift):
    center = values - lax.optimization_barrier(jnp.mean(values, -1, keepdims=True))
    variance = lax.optimization_barrier(jnp.mean(center * center, -1, keepdims=True))
    return center * lax.rsqrt(variance + EPS) * gain + shift

def matmul(left, right):
    return jnp.einsum('csd,de->cse', left, right, precision=lax.Precision.HIGHEST)

def attend(pieces):
    queries, key_rows, value_rows, key_mask = pieces
    q_heads = queries.reshape(SLOTS, HEADS, HEAD_DIM)
    k_heads = key_rows.reshape(SLOTS, HEADS, HEAD_DIM)
    v_heads = value_rows.reshape(SLOTS, HEADS, HEAD_DIM)
    scores = jnp.einsum('qhd,khd->hqk', q_heads, k_heads, precision=lax.Precision.HIGHEST) * 0.125
    scores = low_back(scores)
    scores = jnp.where(key_mask[None, None, :], scores, -1e+30)
    attn_prob = low(jax.nn.softmax(scores, axis=-1))
    mixed = jnp.einsum('hqk,khd->qhd', attn_prob, v_heads, precision=lax.Precision.HIGHEST)
    return mixed.reshape(SLOTS, D)

def forward(tokens, first_gain, first_shift, qkv_weight, query_bias, value_bias, proj_weight, proj_bias, second_gain, second_shift, up_weight, up_bias, down_weight, down_bias, keep, key_mask):
    first_in = low(layer_norm(tokens, first_gain, first_shift))
    projected = matmul(first_in, qkv_weight)
    queries = low(low_back(projected[..., :D] + query_bias))
    key_rows = low(low_back(projected[..., D:2 * D]))
    value_rows = low(low_back(projected[..., 2 * D:] + value_bias))
    attn_rows = lax.map(jax.checkpoint(attend), (queries, key_rows, value_rows, key_mask))
    attn_rows = low(low_back(attn_rows))
    branch = low_back(matmul(attn_rows, proj_weight) + proj_bias)
    mid_rows = tokens + branch
    second_in = low(layer_norm(mid_rows, second_gain, second_shift))
    pre_act = low_back(matmul(second_in, up_weight) + up_bias)
    hidden_rows = low(jax.nn.gelu(pre_act, approximate=False))
    ff_out = low_back(matmul(hidden_rows, down_weight) + down_bias)
    return keep[..., None] * (mid_rows + ff_out)

def reference(tokens, grad_out, freq_keep, lengths, first_gain, first_shift, qkv_weight, query_bias, value_bias, proj_weight, proj_bias, second_gain, second_shift, up_weight, up_bias, down_weight, down_bias):
    columns = jnp.arange(TIME_COLS, dtype=jnp.int32)
    live = (freq_keep[:, :, None] > 0) & (columns[None, None, :] < lengths[:, None, None])
    key_mask = live.reshape(CLIPS, SLOTS)
    keep = key_mask.astype(jnp.float32)
    params = (tokens, first_gain, first_shift, qkv_weight, query_bias, value_bias, proj_weight, proj_bias, second_gain, second_shift, up_weight, up_bias, down_weight, down_bias)
    params = tuple((item.astype(jnp.float32) for item in params))

    def apply_layer(*inputs):
        return forward(*inputs, keep, key_mask)
    block_out, pull_back = jax.vjp(apply_layer, *params)
    grads = pull_back(grad_out.astype(jnp.float32))
    return (block_out.astype(jnp.bfloat16), grads[0].astype(jnp.bfloat16), grads[1], grads[2], grads[3], grads[4], grads[5], grads[6], grads[7], grads[8], grads[9], grads[10], grads[11], grads[12], grads[13])
```

```python
import functools

import jax
import jax.numpy as jnp
from jax import lax
from jax.experimental import pallas as pl
from jax.experimental.pallas import tpu as pltpu
from jax.sharding import PartitionSpec as P

HEADS = 12
HEAD_DIM = 64
TIME_COLS = 99
EPS = 1e-06
F32 = jnp.float32
BF16 = jnp.bfloat16
MESH = pl.DeviceIdType.MESH
NT = (((1,), (1,)), ((), ()))
TN = (((0,), (0,)), ((), ()))
WIN = 256
GROUP = 4


def nt_dot(left, right):
    return lax.dot_general(left, right, NT, preferred_element_type=F32)


def tn_dot(left, right):
    return lax.dot_general(left, right, TN, preferred_element_type=F32)


def dot(left, right):
    return jnp.dot(left, right, preferred_element_type=F32)


def flip(index, stride):
    return index + stride - 2 * stride * ((index // stride) % 2)


def window_start(freq):
    return pl.multiple_of((freq // 2) * 384 + (freq % 2) * 128, 128)


def layer_stats(values):
    center = values - jnp.mean(values, -1, keepdims=True)
    inv_std = lax.rsqrt(jnp.mean(center * center, -1, keepdims=True) + EPS)
    return center * inv_std, inv_std


def head_lanes(core, head):
    lane = lax.broadcasted_iota(jnp.int32, (1, WIN), 1)
    first = 64 * core + 64 * head
    return (lane >= first) & (lane < first + 64)


def spare_lane(core, which):
    lane = lax.broadcasted_iota(jnp.int32, (1, WIN), 1)
    return lane == 192 * (1 - core) + which


def live_rows(shape, freq, keep_ref, length_ref, rows):
    slot = lax.broadcasted_iota(jnp.int32, shape, 0)
    live = jnp.zeros(shape, F32)
    per = rows // TIME_COLS
    for row in range(per):
        column = slot - row * TIME_COLS
        inside = (column >= 0) & (column < TIME_COLS) & (column < length_ref[0])
        kept = (keep_ref[0, freq * per + row] > 0).astype(F32)
        live = jnp.where(inside, kept, live)
    return live


def freq_device(freq):
    return (lax.axis_index("clip"), freq)


def attend_kernel(
    rows, pad, tok_ref, gain_ref, shift_ref, weight_hbm, qbias_ref, vbias_ref, keep_ref, length_ref,
    attn_ref, exp_hbm, q_ref, k_ref, v_ref, out_ref, inv_ref, first_ref, tok_all,
    weight, exp_buf, out_low, attn_in,
    w_sem, e_sem, near_send, near_recv, far_send, far_recv, fwd_send, fwd_recv, out_send, out_recv,
):
    freq = lax.axis_index("freq")
    core = freq % 2
    start = window_start(freq)
    near, far, cross = flip(freq, 1), flip(freq, 2), flip(flip(freq, 1), 2)
    loads = []
    for part in range(3):
        load = pltpu.make_async_copy(
            weight_hbm.at[:, pl.ds(pl.multiple_of(start + 768 * part, 128), WIN)], weight.at[part], w_sem.at[part]
        )
        load.start()
        loads.append(load)
    barrier = pltpu.get_barrier_semaphore()
    for other in (near, far, cross):
        pl.semaphore_signal(barrier, inc=1, device_id=freq_device(other), device_id_type=MESH)
    tok_all[freq, pad - 16 : pad, :] = jnp.zeros((16, 768), BF16)
    tok_all[freq, 0:rows, :] = tok_ref[0]
    pl.semaphore_wait(barrier, 3)

    cuts = [(0, 80), (80, 80), (160, 80), (240, pad - 240)]
    far_copies = []
    for part, (first, count) in enumerate(cuts):
        copy = pltpu.make_async_remote_copy(
            src_ref=tok_all.at[freq, pl.ds(first, count)],
            dst_ref=tok_all.at[freq, pl.ds(first, count)],
            send_sem=far_send.at[part], recv_sem=far_recv.at[part],
            device_id=freq_device(far), device_id_type=MESH,
        )
        copy.start()
        far_copies.append(copy)
    near_copy = pltpu.make_async_remote_copy(
        src_ref=tok_all.at[freq], dst_ref=tok_all.at[freq], send_sem=near_send, recv_sem=near_recv,
        device_id=freq_device(near), device_id_type=MESH,
    )
    near_copy.start()

    def project(slot):
        base = pl.multiple_of(slot * pad, 16)
        span = pl.ds(base, pad)
        normed, _ = layer_stats(tok_all[slot].astype(F32))
        low = (normed * gain_ref[...] + shift_ref[...]).astype(BF16)
        first_ref[span, :] = low
        live = live_rows((pad, 1), slot, keep_ref, length_ref, rows)
        queries = (dot(low, weight[0]) + qbias_ref[:, pl.ds(start, WIN)]).astype(BF16).astype(F32) * 0.125
        keys = dot(low, weight[1])
        values = dot(low, weight[2]) + vbias_ref[:, pl.ds(start, WIN)]
        one = spare_lane(core, 0)
        both = one | spare_lane(core, 1)
        q_ref[span, :] = jnp.where(one, 1.0, queries).astype(BF16)
        k_ref[span, :] = jnp.where(one, (live - 1.0) * 1e30, keys).astype(BF16)
        v_ref[span, :] = jnp.where(both, 1.0, values).astype(BF16)

    for load in loads:
        load.wait()
    project(freq)
    near_copy.wait()
    project(near)
    forwards = []
    for part, (first, count) in enumerate(cuts):
        far_copies[part].wait()
        copy = pltpu.make_async_remote_copy(
            src_ref=tok_all.at[far, pl.ds(first, count)],
            dst_ref=tok_all.at[far, pl.ds(first, count)],
            send_sem=fwd_send.at[part], recv_sem=fwd_recv.at[part],
            device_id=freq_device(near), device_id_type=MESH,
        )
        copy.start()
        forwards.append(copy)
    project(far)
    for copy in forwards:
        copy.wait()
    project(cross)

    sends, saves = [], []
    for turn, slot in enumerate((far, cross, near, freq)):
        base = pl.multiple_of(slot * pad, 16)
        span = pl.ds(base, pad)
        q_rows = q_ref[span, :]
        total = jnp.zeros((pad, WIN), F32)
        inverse = jnp.zeros((pad, WIN), F32)
        for head in range(3):
            lanes = head_lanes(core, head)
            q_head = jnp.where(lanes | spare_lane(core, 0), q_rows, jnp.zeros_like(q_rows))
            scores = nt_dot(q_head, k_ref[...])
            exps = jnp.exp(scores - jnp.max(scores, -1, keepdims=True)).astype(BF16)
            exp_buf[head, span, :] = exps
            mixed = dot(exps, v_ref[...])
            denom = jnp.sum(jnp.where(spare_lane(core, 0), mixed, 0.0), -1, keepdims=True)
            scale = 1.0 / denom
            total = jnp.where(lanes, mixed * scale, total)
            inverse = jnp.where(lanes, scale, inverse)
        save = pltpu.make_async_copy(exp_buf.at[:, span], exp_hbm.at[:, span], e_sem.at[turn])
        save.start()
        saves.append(save)
        out_ref[span, :] = total
        inv_ref[span, :] = inverse
        if turn == 3:
            attn_in[freq] = total.astype(BF16)
        else:
            out_low[span, :] = total.astype(BF16)
            copy = pltpu.make_async_remote_copy(
                src_ref=out_low.at[span], dst_ref=attn_in.at[freq],
                send_sem=out_send.at[turn], recv_sem=out_recv.at[turn],
                device_id=freq_device(slot), device_id_type=MESH,
            )
            copy.start()
            sends.append(copy)
    for copy in sends:
        copy.wait()
    for half in range(2):
        left, right = attn_in[2 * half], attn_in[2 * half + 1]
        at = 384 * half
        attn_ref[:, at : at + 128] = left[:, 0:128]
        attn_ref[:, at + 128 : at + 256] = (left[:, 128:256].astype(F32) + right[:, 0:128].astype(F32)).astype(BF16)
        attn_ref[:, at + 256 : at + 384] = right[:, 128:256]
    for save in saves:
        save.wait()


def attend(tokens, gain, shift, weight, qbias, vbias, keep, lengths):
    rows, width = tokens.shape[1:]
    pad = -(-rows // 16) * 16
    slots = GROUP * pad
    vm = pl.BlockSpec(memory_space=pltpu.VMEM)
    sm = pl.BlockSpec(memory_space=pltpu.SMEM)
    hbm = pl.BlockSpec(memory_space=pl.ANY)
    sd = jax.ShapeDtypeStruct
    dma = pltpu.SemaphoreType.DMA
    return pl.pallas_call(
        functools.partial(attend_kernel, rows, pad),
        out_shape=(
            sd((pad, width), BF16), sd((3, slots, slots), BF16), sd((slots, WIN), BF16), sd((slots, WIN), BF16),
            sd((slots, WIN), BF16), sd((slots, WIN), F32), sd((slots, WIN), F32), sd((slots, width), BF16),
            sd((GROUP, pad, width), BF16),
        ),
        in_specs=[vm, vm, vm, hbm, vm, vm, sm, sm],
        out_specs=[vm, hbm, vm, vm, vm, vm, vm, vm, vm],
        scratch_shapes=[
            pltpu.VMEM((3, width, WIN), BF16), pltpu.VMEM((3, slots, slots), BF16), pltpu.VMEM((slots, WIN), BF16),
            pltpu.VMEM((GROUP, pad, WIN), BF16),
            dma((3,)), dma((4,)), dma, dma, dma((4,)), dma((4,)), dma((4,)), dma((4,)), dma((3,)), dma((3,)),
        ],
        compiler_params=pltpu.CompilerParams(collective_id=0, has_side_effects=True, vmem_limit_bytes=56 << 20),
        name="attend",
    )(tokens, gain.reshape(1, -1), shift.reshape(1, -1), weight, qbias.reshape(1, -1), vbias.reshape(1, -1), keep, lengths)


def norm_back(grad_norm, normed, inv_std, gain):
    scaled = grad_norm * gain
    return inv_std * (
        scaled
        - jnp.mean(scaled, -1, keepdims=True)
        - normed * jnp.mean(scaled * normed, -1, keepdims=True)
    )


def outer_sum(left, right):
    return jnp.einsum("crd,cre->de", left, right, preferred_element_type=jnp.float32)


def column_sum(grad_rows):
    return jnp.sum(grad_rows.astype(jnp.float32), axis=(0, 1))


def back_dot(grad_rows, weight):
    return lax.dot_general(
        grad_rows, weight, (((2,), (1,)), ((), ())), preferred_element_type=jnp.float32
    )


def on_device(
    tokens,
    grad_out,
    freq_keep,
    lengths,
    first_gain,
    first_shift,
    qkv_weight,
    query_bias,
    value_bias,
    proj_weight,
    proj_bias,
    second_gain,
    second_shift,
    up_weight,
    up_bias,
    down_weight,
    down_bias,
):
    clip_count, row_count, model_width = tokens.shape
    head_count = HEADS
    head_size = model_width // head_count
    slot_count = row_count * lax.axis_size("freq")
    columns = jnp.arange(TIME_COLS, dtype=jnp.int32)
    live = (freq_keep[:, :, None] > 0) & (columns[None, None, :] < lengths[:, None, None])
    key_mask = live.reshape(clip_count, slot_count)
    row_start = lax.axis_index("freq") * row_count
    keep = lax.dynamic_slice_in_dim(key_mask, row_start, row_count, 1).astype(jnp.float32)[
        :, :, None
    ]
    inputs = tokens.astype(jnp.float32)
    normed_one, inv_one = layer_stats(inputs)
    first_in = (normed_one * first_gain + first_shift).astype(jnp.bfloat16)
    projected = jnp.dot(first_in, qkv_weight, preferred_element_type=jnp.float32)
    queries = (projected[..., :model_width] + query_bias).astype(jnp.bfloat16)
    key_rows = projected[..., model_width : 2 * model_width].astype(jnp.bfloat16)
    value_rows = (projected[..., 2 * model_width :] + value_bias).astype(jnp.bfloat16)
    key_all, value_all = (
        lax.all_gather(key_rows, "freq", axis=1, tiled=True),
        lax.all_gather(value_rows, "freq", axis=1, tiled=True),
    )

    def head_split(rows_in):
        return rows_in.reshape(rows_in.shape[0], rows_in.shape[1], head_count, head_size)

    q_heads = head_split(queries)

    def scores_of(key_whole):
        raw = (
            jnp.einsum(
                "crhd,cshd->chrs",
                q_heads,
                head_split(key_whole),
                preferred_element_type=jnp.float32,
            )
            * 0.125
        )
        return jnp.where(key_mask[:, None, None, :], raw, -1e30)

    scores = scores_of(key_all)
    row_max = jnp.max(scores, -1, keepdims=True)
    log_total = row_max + jnp.log(jnp.sum(jnp.exp(scores - row_max), -1, keepdims=True))
    attn_rows = attend(
        tokens, first_gain, first_shift, qkv_weight, query_bias, value_bias, freq_keep, lengths
    )[0][None, :row_count]
    mid_rows = inputs + (
        jnp.dot(attn_rows, proj_weight, preferred_element_type=jnp.float32) + proj_bias
    )
    normed_two, inv_two = layer_stats(mid_rows)
    second_in = (normed_two * second_gain + second_shift).astype(jnp.bfloat16)
    pre_act = jnp.dot(second_in, up_weight, preferred_element_type=jnp.float32) + up_bias
    hidden_rows = jax.nn.gelu(pre_act, approximate=False).astype(jnp.bfloat16)
    ff_out = jnp.dot(hidden_rows, down_weight, preferred_element_type=jnp.float32) + down_bias
    block_out = (keep * (mid_rows + ff_out)).astype(jnp.bfloat16)
    grad_kept = keep * grad_out.astype(jnp.float32)
    grad_low = grad_kept.astype(jnp.bfloat16)
    g_down_weight = outer_sum(hidden_rows, grad_low)
    g_down_bias = column_sum(grad_low)
    d_hidden = back_dot(grad_low, down_weight)
    unused_out, gelu_pull = jax.vjp(lambda inner: jax.nn.gelu(inner, approximate=False), pre_act)
    d_pre = gelu_pull(d_hidden)[0].astype(jnp.bfloat16)
    g_up_weight = outer_sum(second_in, d_pre)
    g_up_bias = column_sum(d_pre)
    d_second = back_dot(d_pre, up_weight)
    g_second_gain = jnp.sum(d_second * normed_two, axis=(0, 1))
    g_second_shift = jnp.sum(d_second, axis=(0, 1))
    d_mid = grad_kept + norm_back(d_second, normed_two, inv_two, second_gain)
    d_branch = d_mid.astype(jnp.bfloat16)
    g_proj_weight = outer_sum(attn_rows, d_branch)
    g_proj_bias = column_sum(d_branch)
    d_attn = back_dot(d_branch, proj_weight).astype(jnp.bfloat16)
    key_back, value_back = (key_all, value_all)
    prob_back = jnp.exp(scores_of(key_back) - log_total)
    d_heads = head_split(d_attn)
    d_prob = jnp.einsum(
        "crhd,cshd->chrs", d_heads, head_split(value_back), preferred_element_type=jnp.float32
    )
    d_score = (prob_back * (d_prob - jnp.sum(prob_back * d_prob, -1, keepdims=True))).astype(
        jnp.bfloat16
    )
    d_queries = (
        jnp.einsum(
            "chrs,cshd->crhd", d_score, head_split(key_back), preferred_element_type=jnp.float32
        )
        * 0.125
    )
    d_queries = d_queries.reshape(clip_count, row_count, model_width).astype(jnp.bfloat16)
    d_key_all = (
        jnp.einsum("chrs,crhd->cshd", d_score, q_heads, preferred_element_type=jnp.float32) * 0.125
    )
    d_key_all = d_key_all.reshape(clip_count, slot_count, model_width)
    d_value_all = jnp.einsum(
        "chrs,crhd->cshd",
        prob_back.astype(jnp.bfloat16),
        d_heads,
        preferred_element_type=jnp.float32,
    )
    d_value_all = d_value_all.reshape(clip_count, slot_count, model_width)
    d_key_sum, d_value_sum = (
        lax.psum_scatter(
            d_key_all.astype(jnp.bfloat16), "freq", scatter_dimension=1, tiled=True
        ).astype(jnp.float32),
        lax.psum_scatter(
            d_value_all.astype(jnp.bfloat16), "freq", scatter_dimension=1, tiled=True
        ).astype(jnp.float32),
    )
    d_keys = d_key_sum.astype(jnp.bfloat16)
    d_values = d_value_sum.astype(jnp.bfloat16)
    d_qkv = jnp.concatenate([d_queries, d_keys, d_values], axis=-1)
    g_qkv_weight = outer_sum(first_in, d_qkv)
    g_query_bias = column_sum(d_queries)
    g_value_bias = column_sum(d_values)
    d_first = back_dot(d_qkv, qkv_weight)
    g_first_gain = jnp.sum(d_first * normed_one, axis=(0, 1))
    g_first_shift = jnp.sum(d_first, axis=(0, 1))
    grad_tokens = (d_mid + norm_back(d_first, normed_one, inv_one, first_gain)).astype(jnp.bfloat16)
    every_sum = (
        lax.psum_scatter(g_first_gain, ("clip", "freq"), scatter_dimension=0, tiled=True),
        lax.psum_scatter(g_first_shift, ("clip", "freq"), scatter_dimension=0, tiled=True),
        lax.psum_scatter(g_qkv_weight, ("clip", "freq"), scatter_dimension=0, tiled=True),
        lax.psum_scatter(g_query_bias, ("clip", "freq"), scatter_dimension=0, tiled=True),
        lax.psum_scatter(g_value_bias, ("clip", "freq"), scatter_dimension=0, tiled=True),
        lax.psum_scatter(g_proj_weight, ("clip", "freq"), scatter_dimension=0, tiled=True),
        lax.psum_scatter(g_proj_bias, ("clip", "freq"), scatter_dimension=0, tiled=True),
        lax.psum_scatter(g_up_weight, ("clip", "freq"), scatter_dimension=0, tiled=True),
        lax.psum_scatter(g_up_bias, ("clip", "freq"), scatter_dimension=0, tiled=True),
        lax.psum_scatter(g_down_weight, ("clip", "freq"), scatter_dimension=0, tiled=True),
        lax.psum_scatter(g_down_bias, ("clip", "freq"), scatter_dimension=0, tiled=True),
        lax.psum_scatter(g_second_gain, ("clip", "freq"), scatter_dimension=0, tiled=True),
        lax.psum_scatter(g_second_shift, ("clip", "freq"), scatter_dimension=0, tiled=True),
    )
    (
        sum_first_gain,
        sum_first_shift,
        sum_qkv_weight,
        sum_query_bias,
        sum_value_bias,
        sum_proj_weight,
        sum_proj_bias,
        sum_up_weight,
        sum_up_bias,
        sum_down_weight,
        sum_down_bias,
        sum_second_gain,
        sum_second_shift,
    ) = every_sum
    return (
        block_out,
        grad_tokens,
        sum_first_gain,
        sum_first_shift,
        sum_qkv_weight,
        sum_query_bias,
        sum_value_bias,
        sum_proj_weight,
        sum_proj_bias,
        sum_second_gain,
        sum_second_shift,
        sum_up_weight,
        sum_up_bias,
        sum_down_weight,
        sum_down_bias,
    )


def solution(mesh):
    placed = (
        P("clip", "freq", None),
        P("clip", "freq", None),
        P("clip", None),
        P("clip"),
        P(),
        P(),
        P(),
        P(),
        P(),
        P(),
        P(),
        P(),
        P(),
        P(),
        P(),
        P(),
        P(),
    )
    return jax.shard_map(
        on_device,
        mesh=mesh,
        in_specs=placed,
        out_specs=(
            P("clip", "freq", None),
            P("clip", "freq", None),
            P(("clip", "freq")),
            P(("clip", "freq")),
            P(("clip", "freq"), None),
            P(("clip", "freq")),
            P(("clip", "freq")),
            P(("clip", "freq"), None),
            P(("clip", "freq")),
            P(("clip", "freq")),
            P(("clip", "freq")),
            P(("clip", "freq"), None),
            P(("clip", "freq")),
            P(("clip", "freq"), None),
            P(("clip", "freq")),
        ),
        check_vma=False,
    )
```

```python
import functools
import types

import jax
import jax.numpy as jnp
from jax import lax
from jax.experimental import pallas as pl
from jax.experimental.pallas import tpu as pltpu
from jax.sharding import PartitionSpec as P

HEADS = 12
HEAD_DIM = 64
TIME_COLS = 99
EPS = 1e-06
F32 = jnp.float32
BF16 = jnp.bfloat16
MESH = pl.DeviceIdType.MESH
NT = (((1,), (1,)), ((), ()))
TN = (((0,), (0,)), ((), ()))
WIN = 256
GROUP = 4


def nt_dot(left, right):
    return lax.dot_general(left, right, NT, preferred_element_type=F32)


def tn_dot(left, right):
    return lax.dot_general(left, right, TN, preferred_element_type=F32)


def dot(left, right):
    return jnp.dot(left, right, preferred_element_type=F32)


def flip(index, stride):
    return index + stride - 2 * stride * ((index // stride) % 2)


def window_start(freq):
    return pl.multiple_of((freq // 2) * 384 + (freq % 2) * 128, 128)


def layer_stats(values):
    center = values - jnp.mean(values, -1, keepdims=True)
    inv_std = lax.rsqrt(jnp.mean(center * center, -1, keepdims=True) + EPS)
    return center * inv_std, inv_std


def head_lanes(core, head):
    lane = lax.broadcasted_iota(jnp.int32, (1, WIN), 1)
    first = 64 * core + 64 * head
    return (lane >= first) & (lane < first + 64)


def spare_lane(core, which):
    lane = lax.broadcasted_iota(jnp.int32, (1, WIN), 1)
    return lane == 192 * (1 - core) + which


def live_rows(shape, freq, keep_ref, length_ref, rows):
    slot = lax.broadcasted_iota(jnp.int32, shape, 0)
    live = jnp.zeros(shape, F32)
    per = rows // TIME_COLS
    for row in range(per):
        column = slot - row * TIME_COLS
        inside = (column >= 0) & (column < TIME_COLS) & (column < length_ref[0])
        kept = (keep_ref[0, freq * per + row] > 0).astype(F32)
        live = jnp.where(inside, kept, live)
    return live


def freq_device(freq):
    return (lax.axis_index("clip"), freq)


def attend_kernel(
    rows, pad, tok_ref, gain_ref, shift_ref, weight_hbm, qbias_ref, vbias_ref, keep_ref, length_ref,
    attn_ref, exp_hbm, q_ref, k_ref, v_ref, out_ref, inv_ref, first_ref, tok_all,
    weight, exp_buf, out_low, attn_in,
    w_sem, e_sem, near_send, near_recv, far_send, far_recv, fwd_send, fwd_recv, out_send, out_recv,
):
    freq = lax.axis_index("freq")
    core = freq % 2
    start = window_start(freq)
    near, far, cross = flip(freq, 1), flip(freq, 2), flip(flip(freq, 1), 2)
    loads = []
    for part in range(3):
        load = pltpu.make_async_copy(
            weight_hbm.at[:, pl.ds(pl.multiple_of(start + 768 * part, 128), WIN)], weight.at[part], w_sem.at[part]
        )
        load.start()
        loads.append(load)
    barrier = pltpu.get_barrier_semaphore()
    for other in (near, far, cross):
        pl.semaphore_signal(barrier, inc=1, device_id=freq_device(other), device_id_type=MESH)
    tok_all[freq, pad - 16 : pad, :] = jnp.zeros((16, 768), BF16)
    tok_all[freq, 0:rows, :] = tok_ref[0]
    pl.semaphore_wait(barrier, 3)

    cuts = [(0, 80), (80, 80), (160, 80), (240, pad - 240)]
    far_copies = []
    for part, (first, count) in enumerate(cuts):
        copy = pltpu.make_async_remote_copy(
            src_ref=tok_all.at[freq, pl.ds(first, count)],
            dst_ref=tok_all.at[freq, pl.ds(first, count)],
            send_sem=far_send.at[part], recv_sem=far_recv.at[part],
            device_id=freq_device(far), device_id_type=MESH,
        )
        copy.start()
        far_copies.append(copy)
    near_copy = pltpu.make_async_remote_copy(
        src_ref=tok_all.at[freq], dst_ref=tok_all.at[freq], send_sem=near_send, recv_sem=near_recv,
        device_id=freq_device(near), device_id_type=MESH,
    )
    near_copy.start()

    def project(slot):
        base = pl.multiple_of(slot * pad, 16)
        span = pl.ds(base, pad)
        normed, _ = layer_stats(tok_all[slot].astype(F32))
        low = (normed * gain_ref[...] + shift_ref[...]).astype(BF16)
        first_ref[span, :] = low
        live = live_rows((pad, 1), slot, keep_ref, length_ref, rows)
        queries = (dot(low, weight[0]) + qbias_ref[:, pl.ds(start, WIN)]).astype(BF16).astype(F32) * 0.125
        keys = dot(low, weight[1])
        values = dot(low, weight[2]) + vbias_ref[:, pl.ds(start, WIN)]
        one = spare_lane(core, 0)
        both = one | spare_lane(core, 1)
        q_ref[span, :] = jnp.where(one, 1.0, queries).astype(BF16)
        k_ref[span, :] = jnp.where(one, (live - 1.0) * 1e30, keys).astype(BF16)
        v_ref[span, :] = jnp.where(both, 1.0, values).astype(BF16)

    for load in loads:
        load.wait()
    project(freq)
    near_copy.wait()
    project(near)
    forwards = []
    for part, (first, count) in enumerate(cuts):
        far_copies[part].wait()
        copy = pltpu.make_async_remote_copy(
            src_ref=tok_all.at[far, pl.ds(first, count)],
            dst_ref=tok_all.at[far, pl.ds(first, count)],
            send_sem=fwd_send.at[part], recv_sem=fwd_recv.at[part],
            device_id=freq_device(near), device_id_type=MESH,
        )
        copy.start()
        forwards.append(copy)
    project(far)
    for copy in forwards:
        copy.wait()
    project(cross)

    sends, saves = [], []
    for turn, slot in enumerate((far, cross, near, freq)):
        base = pl.multiple_of(slot * pad, 16)
        span = pl.ds(base, pad)
        q_rows = q_ref[span, :]
        total = jnp.zeros((pad, WIN), F32)
        inverse = jnp.zeros((pad, WIN), F32)
        for head in range(3):
            lanes = head_lanes(core, head)
            q_head = jnp.where(lanes | spare_lane(core, 0), q_rows, jnp.zeros_like(q_rows))
            scores = nt_dot(q_head, k_ref[...])
            exps = jnp.exp(scores - jnp.max(scores, -1, keepdims=True)).astype(BF16)
            exp_buf[head, span, :] = exps
            mixed = dot(exps, v_ref[...])
            denom = jnp.sum(jnp.where(spare_lane(core, 0), mixed, 0.0), -1, keepdims=True)
            scale = 1.0 / denom
            total = jnp.where(lanes, mixed * scale, total)
            inverse = jnp.where(lanes, scale, inverse)
        save = pltpu.make_async_copy(exp_buf.at[:, span], exp_hbm.at[:, span], e_sem.at[turn])
        save.start()
        saves.append(save)
        out_ref[span, :] = total
        inv_ref[span, :] = inverse
        if turn == 3:
            attn_in[freq] = total.astype(BF16)
        else:
            out_low[span, :] = total.astype(BF16)
            copy = pltpu.make_async_remote_copy(
                src_ref=out_low.at[span], dst_ref=attn_in.at[freq],
                send_sem=out_send.at[turn], recv_sem=out_recv.at[turn],
                device_id=freq_device(slot), device_id_type=MESH,
            )
            copy.start()
            sends.append(copy)
    for copy in sends:
        copy.wait()
    for half in range(2):
        left, right = attn_in[2 * half], attn_in[2 * half + 1]
        at = 384 * half
        attn_ref[:, at : at + 128] = left[:, 0:128]
        attn_ref[:, at + 128 : at + 256] = (left[:, 128:256].astype(F32) + right[:, 0:128].astype(F32)).astype(BF16)
        attn_ref[:, at + 256 : at + 384] = right[:, 128:256]
    for save in saves:
        save.wait()


def attend(tokens, gain, shift, weight, qbias, vbias, keep, lengths):
    rows, width = tokens.shape[1:]
    pad = -(-rows // 16) * 16
    slots = GROUP * pad
    vm = pl.BlockSpec(memory_space=pltpu.VMEM)
    sm = pl.BlockSpec(memory_space=pltpu.SMEM)
    hbm = pl.BlockSpec(memory_space=pl.ANY)
    sd = jax.ShapeDtypeStruct
    dma = pltpu.SemaphoreType.DMA
    return pl.pallas_call(
        functools.partial(attend_kernel, rows, pad),
        out_shape=(
            sd((pad, width), BF16), sd((3, slots, slots), BF16), sd((slots, WIN), BF16), sd((slots, WIN), BF16),
            sd((slots, WIN), BF16), sd((slots, WIN), F32), sd((slots, WIN), F32), sd((slots, width), BF16),
            sd((GROUP, pad, width), BF16),
        ),
        in_specs=[vm, vm, vm, hbm, vm, vm, sm, sm],
        out_specs=[vm, hbm, vm, vm, vm, vm, vm, vm, vm],
        scratch_shapes=[
            pltpu.VMEM((3, width, WIN), BF16), pltpu.VMEM((3, slots, slots), BF16), pltpu.VMEM((slots, WIN), BF16),
            pltpu.VMEM((GROUP, pad, WIN), BF16),
            dma((3,)), dma((4,)), dma, dma, dma((4,)), dma((4,)), dma((4,)), dma((4,)), dma((3,)), dma((3,)),
        ],
        compiler_params=pltpu.CompilerParams(collective_id=0, has_side_effects=True, vmem_limit_bytes=56 << 20),
        name="attend",
    )(tokens, gain.reshape(1, -1), shift.reshape(1, -1), weight, qbias.reshape(1, -1), vbias.reshape(1, -1), keep, lengths)


class Transfers:
    def __init__(self, local_sem, send_sem, recv_sem):
        self.local_sem, self.send_sem, self.recv_sem = local_sem, send_sem, recv_sem
        self.locals, self.remotes = 0, 0

    def load(self, source, target):
        copy = pltpu.make_async_copy(source, target, self.local_sem.at[self.locals])
        self.locals += 1
        copy.start()
        return copy

    def send(self, source, target, device):
        copy = pltpu.make_async_remote_copy(
            src_ref=source, dst_ref=target, send_sem=self.send_sem.at[self.remotes],
            recv_sem=self.recv_sem.at[self.remotes], device_id=device, device_id_type=MESH,
        )
        self.remotes += 1
        copy.start()
        return copy


def column_total(values):
    return jnp.sum(values, axis=0, keepdims=True)


def add_low(left, right):
    return (left.astype(F32) + right.astype(F32)).astype(BF16)


def layer_kernel(names, rows, pad, fast, *refs):
    r = types.SimpleNamespace(**dict(zip(names, refs)))
    clip, freq = lax.axis_index("clip"), lax.axis_index("freq")
    core, side = freq % 2, freq // 2
    near, far, cross = flip(freq, 1), flip(freq, 2), flip(flip(freq, 1), 2)
    x_bit, z_low, z_high = clip % 2, (clip // 2) % 2, clip // 4
    to_near, to_far, to_cross = (clip, near), (clip, far), (clip, cross)
    to_x, to_zl, to_zh = (flip(clip, 1), freq), (flip(clip, 2), freq), (flip(clip, 4), freq)
    slots = GROUP * pad
    pair = 2 * pad
    half = 384
    t = Transfers(r.local_sem, r.send_sem, r.recv_sem)
    mine = pl.ds(pl.multiple_of(core * pad, 16), pad)
    my_half = pl.ds(pl.multiple_of(core * half, 128), half)
    near_half = pl.ds(pl.multiple_of((1 - core) * half, 128), half)
    start = window_start(freq)
    window = pl.ds(start, WIN)

    def load_chunk(chunk):
        cut = pl.ds(768 * chunk, 768)
        return (
            t.load(r.up_hbm.at[:, cut], r.up_buf.at[chunk % 2]),
            t.load(r.down_hbm.at[cut, :], r.down_buf.at[chunk % 2]),
        )

    load_proj = t.load(r.proj_hbm, r.proj)
    chunk_loads = [load_chunk(0), load_chunk(1)]
    late_loads = [
        t.load(source, target)
        for source, target in (
            (r.q_hbm, r.q), (r.k_hbm, r.k), (r.v_hbm, r.v), (r.inv_hbm, r.inv), (r.out_hbm, r.out),
            (r.first_hbm, r.first), (r.tok_hbm, r.tok),
        )
    ]
    partners = [to_near, to_far, to_cross] + ([to_x, to_zl, to_zh] if fast else [])
    barrier = pltpu.get_barrier_semaphore()
    for device in partners:
        pl.semaphore_signal(barrier, inc=1, device_id=device, device_id_type=MESH)

    keep = live_rows((pad, 1), freq, r.keep_ref, r.length_ref, rows)
    r.mid[pad - 16 : pad, :] = jnp.zeros((16, 768), F32)
    r.mid[0:rows, :] = r.tok_ref[0].astype(F32)
    r.grad[pad - 16 : pad, :] = jnp.zeros((16, 768), BF16)
    r.grad[0:rows, :] = r.grad_ref[0]
    r.grad[...] = (r.grad[...].astype(F32) * keep).astype(BF16)
    r.vec[...] = jnp.zeros_like(r.vec)
    r.dkt[...] = jnp.zeros_like(r.dkt)
    r.dvt[...] = jnp.zeros_like(r.dvt)
    pl.semaphore_wait(barrier, len(partners))

    r.grad2[mine, :] = r.grad[:, my_half]
    send_grad = t.send(r.grad.at[:, near_half], r.grad2.at[mine], to_near)
    r.att2[mine, :] = r.attn_ref[...]
    send_att = t.send(r.att2.at[mine], r.att2.at[mine], to_near)

    load_proj.wait()
    middle = r.mid[...] + (dot(r.attn_ref[...], r.proj[...]) + r.proj_bias[...])
    r.mid[...] = middle
    normed, inv_two = layer_stats(middle)
    r.normed[...] = normed
    r.inv_two[...] = inv_two
    r.sec2[mine, :] = (normed * r.second_gain[...] + r.second_shift[...]).astype(BF16)
    send_sec = t.send(r.sec2.at[mine], r.sec2.at[mine], to_near)

    hid_sends, pre_sends = [None] * 4, [None] * 4
    down_x, up_y = [None] * 4, [None] * 5

    def send_up(chunk):
        if fast:
            up_y[chunk] = t.send(r.g_up.at[chunk, :, :, :, 1 - side], r.up_y.at[chunk], to_far)

    def weight_part(chunk):
        slot = chunk % 2
        hid_sends[chunk].wait()
        g_down = tn_dot(r.hid2[slot], r.grad2[...]).astype(BF16)
        r.g_down[chunk // 2, chunk % 2] = g_down.reshape(2, 2, 192, half)
        if fast:
            down_x[chunk] = t.send(
                r.g_down.at[chunk // 2, chunk % 2, 1 - x_bit], r.down_x.at[chunk // 2, chunk % 2], to_x
            )
        pre_sends[chunk].wait()
        g_up = tn_dot(r.sec2[...], r.pre2[slot]).astype(BF16)
        r.g_up[chunk] = g_up.reshape(2, 2, 2, 2, 48, half)

    for chunk in range(4):
        slot = chunk % 2
        cut = slice(768 * chunk, 768 * chunk + 768)
        for load in chunk_loads[chunk]:
            load.wait()
        up, down = r.up_buf[slot], r.down_buf[slot]
        inner = dot(r.sec2[mine, :], up) + r.up_bias[:, cut]
        share = 0.5 * (1.0 + lax.erf(inner * 0.7071067811865476))
        hidden = (inner * share).astype(BF16)
        slope = share + inner * (0.3989422804014327 * jnp.exp(-0.5 * inner * inner))
        r.hid2[slot, mine, :] = hidden
        more = dot(hidden, down)
        d_pre = (nt_dot(r.grad[...], down) * slope).astype(BF16)
        r.pre_out[slot] = d_pre
        r.vec[8 + chunk : 9 + chunk, :] = column_total(d_pre.astype(F32))
        back = nt_dot(d_pre, up)
        if chunk == 0:
            r.ff[...] = more
            r.dsec[...] = back
        else:
            r.ff[...] += more
            r.dsec[...] += back
        if chunk + 2 < 4:
            chunk_loads.append(load_chunk(chunk + 2))
        if chunk == 0:
            send_grad.wait()
            send_sec.wait()
        else:
            weight_part(chunk - 1)
            if chunk < 3:
                send_up(chunk - 1)
        r.pre2[slot, mine, :] = r.pre_out[slot, :, my_half]
        hid_sends[chunk] = t.send(r.hid2.at[slot, mine], r.hid2.at[slot, mine], to_near)
        pre_sends[chunk] = t.send(r.pre_out.at[slot, :, near_half], r.pre2.at[slot, mine], to_near)

    load_wide = [
        t.load(r.qkv_hbm.at[:, pl.ds(pl.multiple_of(start + 768 * part, 128), WIN)], r.up_buf.at[0, :, pl.ds(WIN * part, WIN)])
        for part in range(3)
    ]
    d_second = r.dsec[...]
    r.vec[5:6, :] = column_total(d_second * r.normed[...])
    r.vec[6:7, :] = column_total(d_second)
    scaled = d_second * r.second_gain[...]
    grad_rows = r.grad[...].astype(F32)
    r.vec[7:8, :] = column_total(grad_rows)
    d_mid = grad_rows + r.inv_two[...] * (
        scaled
        - jnp.mean(scaled, -1, keepdims=True)
        - r.normed[...] * jnp.mean(scaled * r.normed[...], -1, keepdims=True)
    )
    r.dsec[...] = d_mid
    branch = d_mid.astype(BF16)
    r.vec[4:5, :] = column_total(branch.astype(F32))
    r.branch[...] = branch
    r.dattn[...] = nt_dot(branch, r.proj[...]).astype(BF16)
    attn_sends = [
        t.send(r.dattn.at[:, pl.ds(window_start(other), WIN)], r.dout.at[freq], (clip, other))
        for other in (far, cross, near)
    ]
    r.branch2[mine, :] = r.branch[:, my_half]
    send_branch = t.send(r.branch.at[:, near_half], r.branch2.at[mine], to_near)
    r.dout[freq] = r.dattn[:, window]
    r.block_out[...] = (keep * (r.mid[...] + (r.ff[...] + r.down_bias[...]))).astype(BF16)
    weight_part(3)
    send_up(2)
    send_up(3)
    send_att.wait()
    send_branch.wait()
    r.g_up[4] = tn_dot(r.att2[...], r.branch2[...]).astype(BF16).reshape(2, 2, 2, 2, 48, half)
    send_up(4)

    blocks = (side, 1 - side)
    exp_loads = [None] * 6

    def load_exp(step):
        at = pl.ds(pl.multiple_of(blocks[step // 3] * pair, 16), pair)
        exp_loads[step] = t.load(r.exp_hbm.at[step % 3, at], r.exps.at[step % 3])

    for step in range(3):
        load_exp(step)
    for load in late_loads:
        load.wait()
    head_rows = [pl.ds(pl.multiple_of(64 * core + 64 * head, 64), 64) for head in range(3)]
    for turn in range(2):
        block = blocks[turn]
        at = pl.ds(pl.multiple_of(block * pair, 16), pair)
        if turn == 0:
            attn_sends[2].wait()
        else:
            attn_sends[0].wait()
            attn_sends[1].wait()
        grads = jnp.concatenate([r.dout[2 * block].astype(F32), r.dout[2 * block + 1].astype(F32)], axis=0) * r.inv[at, :]
        r.dscaled[...] = grads.astype(BF16)
        r.qt[...] = r.q[at, :].astype(F32).T.astype(BF16)
        r.dot_t[...] = grads.T.astype(BF16)
        products = grads * r.out[at, :]
        dq_total = jnp.zeros((pair, WIN), F32)
        for head in range(3):
            step = 3 * turn + head
            lanes = head_lanes(core, head)
            mean = jnp.sum(jnp.where(lanes, products, 0.0), -1, keepdims=True)
            high = mean.astype(BF16).astype(F32)
            fill = jnp.where(spare_lane(core, 0), -high, jnp.where(spare_lane(core, 1), high - mean, 0.0))
            d_head = jnp.where(lanes, r.dscaled[...].astype(F32), fill).astype(BF16)
            exp_loads[step].wait()
            exps = r.exps[head]
            d_prob = nt_dot(d_head, r.v[...])
            d_score = (exps.astype(F32) * d_prob).astype(BF16)
            dq_total = jnp.where(lanes, dot(d_score, r.k[...]), dq_total)
            r.dkt[head_rows[head], :] += dot(r.qt[head_rows[head], :], d_score)
            r.dvt[head_rows[head], :] += dot(r.dot_t[head_rows[head], :], exps)
            if turn == 0:
                load_exp(step + 3)
        r.dqkv[at, 0:WIN] = (dq_total * 0.125).astype(BF16)
        if fast and turn == 0:
            for chunk in range(2):
                up_y[chunk].wait()
                r.up_y[chunk] = add_low(r.up_y[chunk], r.g_up[chunk, :, :, :, side])
            up_x = [t.send(r.up_y.at[chunk, :, :, 1 - x_bit], r.up_x.at[chunk], to_x) for chunk in range(2)]
            for chunk in range(4):
                down_x[chunk].wait()
                r.down_x[chunk // 2, chunk % 2] = add_low(
                    r.down_x[chunk // 2, chunk % 2], r.g_down[chunk // 2, chunk % 2, x_bit]
                )
            down_zl = t.send(r.down_x.at[:, 1 - z_low], r.down_zl, to_zl)
    r.dqkv[:, WIN : 2 * WIN] = r.dkt[...].T.astype(BF16)
    r.dqkv[:, 2 * WIN : 3 * WIN] = r.dvt[...].T.astype(BF16)
    r.vec[2:3, window] = column_total(r.dqkv[:, 0:WIN].astype(F32))
    r.vec[3:4, window] = column_total(r.dqkv[:, 2 * WIN : 3 * WIN].astype(F32))

    for load in load_wide:
        load.wait()

    def first_back(slot):
        at = pl.ds(pl.multiple_of(slot * pad, 16), pad)
        d_first = nt_dot(r.dqkv[at, :], r.up_buf[0])
        normed_one, inv_one = layer_stats(r.tok[slot].astype(F32))
        r.vec[0:1, :] += column_total(d_first * normed_one)
        r.vec[1:2, :] += column_total(d_first)
        return d_first, normed_one, inv_one

    for turn, slot in enumerate((near, cross)):
        r.first_out[turn] = first_back(slot)[0].astype(BF16)
    send_first = t.send(r.first_out, r.first_near, to_near)
    for part in range(3):
        cut = slice(WIN * part, WIN * part + WIN)
        g_qkv = tn_dot(r.first[...], r.dqkv[:, cut]).astype(BF16)
        r.g_qkv[part] = g_qkv.reshape(2, 2, 2, 96, WIN)
    if fast:
        qkv_x = [t.send(r.g_qkv.at[part, :, :, 1 - x_bit], r.qkv_x.at[part], to_x) for part in range(3)]
    own_first, normed_one, inv_one = first_back(freq)
    far_first = first_back(far)[0]
    send_first.wait()
    r.far_out[...] = (far_first + r.first_near[1].astype(F32)).astype(BF16)
    send_far = t.send(r.far_out, r.first_far, to_far)
    r.ff[...] = own_first + r.first_near[0].astype(F32)

    if fast:
        for index in range(32):
            turned = pltpu.roll(r.vec[0:8, :], (768 - 24 * index) % 768, 1)
            at = (index // 16, (index // 8) % 2, (index // 4) % 2, (index // 2) % 2, index % 2)
            r.small[at + (slice(0, 8), slice(None))] = turned[:, 0:128]
            biases = pltpu.roll(r.vec[8:16, :], (768 - 96 * (index % 8)) % 768, 1)
            r.small[at + (slice(8, 16), slice(None))] = biases[:, 0:128]
        small_c = t.send(r.small.at[:, :, :, :, 1 - core], r.small_c, to_near)
        for chunk in range(2, 5):
            up_y[chunk].wait()
            r.up_y[chunk] = add_low(r.up_y[chunk], r.g_up[chunk, :, :, :, side])
            up_x.append(t.send(r.up_y.at[chunk, :, :, 1 - x_bit], r.up_x.at[chunk], to_x))
        small_c.wait()
        r.small_c[...] += r.small[:, :, :, :, core]
        small_y = t.send(r.small_c.at[:, :, :, 1 - side], r.small_y, to_far)
        down_zl.wait()
        r.down_zl[...] = add_low(r.down_zl[...], r.down_x[:, z_low])
        down_zh = t.send(r.down_zl.at[1 - z_high], r.down_zh, to_zh)
        small_y.wait()
        r.small_y[...] += r.small_c[:, :, :, side]
        small_x = t.send(r.small_y.at[:, :, 1 - x_bit], r.small_x, to_x)
        down_zh.wait()
        r.down_zh[...] = add_low(r.down_zh[...], r.down_zl[z_high])
        down_y = t.send(r.down_zh.at[1 - side], r.down_y, to_far)
        up_zl, qkv_zl = [], []
        for chunk in range(5):
            up_x[chunk].wait()
            r.up_x[chunk] = add_low(r.up_x[chunk], r.up_y[chunk, :, :, x_bit])
            up_zl.append(t.send(r.up_x.at[chunk, :, 1 - z_low], r.up_zl.at[chunk], to_zl))
        small_x.wait()
        r.small_x[...] += r.small_y[:, :, x_bit]
        small_zl = t.send(r.small_x.at[:, 1 - z_low], r.small_zl, to_zl)
        for part in range(3):
            qkv_x[part].wait()
            r.qkv_x[part] = add_low(r.qkv_x[part], r.g_qkv[part, :, :, x_bit])
            qkv_zl.append(t.send(r.qkv_x.at[part, :, 1 - z_low], r.qkv_zl.at[part], to_zl))
        up_zh, qkv_zh = [], []
        for chunk in range(5):
            up_zl[chunk].wait()
            r.up_zl[chunk] = add_low(r.up_zl[chunk], r.up_x[chunk, :, z_low])
            up_zh.append(t.send(r.up_zl.at[chunk, 1 - z_high], r.up_zh.at[chunk], to_zh))
        small_zl.wait()
        r.small_zl[...] += r.small_x[:, z_low]
        small_zh = t.send(r.small_zl.at[1 - z_high], r.small_zh, to_zh)
        for part in range(3):
            qkv_zl[part].wait()
            r.qkv_zl[part] = add_low(r.qkv_zl[part], r.qkv_x[part, :, z_low])
            qkv_zh.append(t.send(r.qkv_zl.at[part, 1 - z_high], r.qkv_zh.at[part], to_zh))
        down_y.wait()
        r.down_fin[...] = r.down_y[...].astype(F32).reshape(2, 96, half) + r.down_zh[side].astype(F32).reshape(2, 96, half)
        down_c = t.send(r.down_fin.at[1 - core], r.down_c, to_near)
        for chunk in range(5):
            up_zh[chunk].wait()
            r.up_fin[chunk] = (r.up_zh[chunk].astype(F32) + r.up_zl[chunk, z_high].astype(F32)).reshape(2, 24, half)
        up_c = t.send(r.up_fin.at[:, 1 - core], r.up_c, to_near)
        for part in range(3):
            qkv_zh[part].wait()
            total = r.qkv_zh[part].astype(F32) + r.qkv_zl[part, z_high].astype(F32)
            r.qkv_fin[:, :, WIN * part : WIN * part + WIN] = total.reshape(4, 24, WIN)
        qkv_c = [t.send(r.qkv_fin.at[other], r.qkv_c.at[freq], (clip, other)) for other in (far, cross, near)]
        r.qkv_c[freq] = r.qkv_fin[freq]

    send_far.wait()
    d_first = r.ff[...] + r.first_far[...].astype(F32)
    scaled = d_first * r.first_gain[...]
    r.grad_tok[...] = (
        r.dsec[...]
        + inv_one
        * (
            scaled
            - jnp.mean(scaled, -1, keepdims=True)
            - normed_one * jnp.mean(scaled * normed_one, -1, keepdims=True)
        )
    ).astype(BF16)

    if fast:
        small_zh.wait()
        r.small_fin[...] = r.small_zh[...] + r.small_zl[z_high]
        down_c.wait()
        r.down_grad[:, my_half] = r.down_fin[core]
        r.down_grad[:, near_half] = r.down_c[...]
        up_c.wait()
        for chunk in range(5):
            place = r.up_grad if chunk < 4 else r.proj_grad
            base = 768 * (chunk % 4)
            place[:, pl.ds(pl.multiple_of(base + half * core, 128), half)] = r.up_fin[chunk, core]
            place[:, pl.ds(pl.multiple_of(base + half * (1 - core), 128), half)] = r.up_c[chunk]
        for copy in qkv_c:
            copy.wait()
        for part in range(3):
            for other in range(2):
                left = r.qkv_c[2 * other, :, WIN * part : WIN * part + WIN]
                right = r.qkv_c[2 * other + 1, :, WIN * part : WIN * part + WIN]
                base = 768 * part + 384 * other
                r.qkv_grad[:, base : base + 128] = left[:, 0:128]
                r.qkv_grad[:, base + 128 : base + 256] = left[:, 128:256] + right[:, 0:128]
                r.qkv_grad[:, base + 256 : base + 384] = right[:, 128:256]


def layer_call(fast, tokens, grad_out, keep, lengths, vectors, weights, saved):
    rows, width = tokens.shape[1:]
    pad = -(-rows // 16) * 16
    slots, pair, half = GROUP * pad, 2 * pad, width // 2
    wide = 4 * width
    sd, vm = jax.ShapeDtypeStruct, pltpu.VMEM
    in_vm, in_sm, in_hbm = pl.BlockSpec(memory_space=pltpu.VMEM), pl.BlockSpec(memory_space=pltpu.SMEM), pl.BlockSpec(memory_space=pl.ANY)
    ins = {
        "tok_ref": (tokens, in_vm), "grad_ref": (grad_out, in_vm), "keep_ref": (keep, in_sm), "length_ref": (lengths, in_sm),
    }
    for name, value in vectors.items():
        ins[name] = (value.reshape(1, -1), in_vm)
    for name, value in weights.items():
        ins[name] = (value, in_hbm)
    for name, value in saved.items():
        ins[name] = (value, in_vm if name == "attn_ref" else in_hbm)
    outs = {"block_out": sd((pad, width), BF16), "grad_tok": sd((pad, width), BF16)}
    if fast:
        outs.update(
            qkv_grad=sd((24, 3 * width), F32), proj_grad=sd((24, width), F32), up_grad=sd((24, wide), F32),
            down_grad=sd((96, width), F32), small_fin=sd((16, 128), F32),
        )
    else:
        outs.update(
            g_qkv=sd((3, 2, 2, 2, 96, WIN), BF16), g_up=sd((5, 2, 2, 2, 2, 48, half), BF16),
            g_down=sd((2, 2, 2, 2, 192, half), BF16), vec=sd((16, width), F32),
        )
    scratch = {
        "proj": vm((width, width), BF16), "up_buf": vm((2, width, width), BF16), "down_buf": vm((2, width, width), BF16),
        "q": vm((slots, WIN), BF16), "k": vm((slots, WIN), BF16), "v": vm((slots, WIN), BF16),
        "inv": vm((slots, WIN), F32), "out": vm((slots, WIN), F32), "first": vm((slots, width), BF16),
        "tok": vm((GROUP, pad, width), BF16),
        "mid": vm((pad, width), F32), "grad": vm((pad, width), BF16), "normed": vm((pad, width), F32),
        "inv_two": vm((pad, 1), F32), "ff": vm((pad, width), F32), "dsec": vm((pad, width), F32),
        "grad2": vm((pair, half), BF16), "att2": vm((pair, width), BF16), "sec2": vm((pair, width), BF16),
        "hid2": vm((2, pair, width), BF16), "pre2": vm((2, pair, half), BF16), "pre_out": vm((2, pad, width), BF16),
        "branch": vm((pad, width), BF16), "branch2": vm((pair, half), BF16), "dattn": vm((pad, width), BF16),
        "dout": vm((GROUP, pad, WIN), BF16), "dscaled": vm((pair, WIN), BF16), "qt": vm((WIN, pair), BF16),
        "dot_t": vm((WIN, pair), BF16), "exps": vm((3, pair, slots), BF16), "dkt": vm((WIN, slots), F32),
        "dvt": vm((WIN, slots), F32), "dqkv": vm((slots, width), BF16), "first_out": vm((2, pad, width), BF16),
        "first_near": vm((2, pad, width), BF16), "far_out": vm((pad, width), BF16), "first_far": vm((pad, width), BF16),
    }
    if fast:
        scratch.update(
            vec=vm((16, width), F32),
            g_down=vm((2, 2, 2, 2, 192, half), BF16), down_x=vm((2, 2, 2, 192, half), BF16), down_zl=vm((2, 2, 192, half), BF16),
            down_zh=vm((2, 192, half), BF16), down_y=vm((192, half), BF16), down_fin=vm((2, 96, half), F32), down_c=vm((96, half), F32),
            g_up=vm((5, 2, 2, 2, 2, 48, half), BF16), up_y=vm((5, 2, 2, 2, 48, half), BF16), up_x=vm((5, 2, 2, 48, half), BF16),
            up_zl=vm((5, 2, 48, half), BF16), up_zh=vm((5, 48, half), BF16), up_fin=vm((5, 2, 24, half), F32), up_c=vm((5, 24, half), F32),
            g_qkv=vm((3, 2, 2, 2, 96, WIN), BF16), qkv_x=vm((3, 2, 2, 96, WIN), BF16), qkv_zl=vm((3, 2, 96, WIN), BF16),
            qkv_zh=vm((3, 96, WIN), BF16), qkv_fin=vm((4, 24, 3 * WIN), F32), qkv_c=vm((4, 24, 3 * WIN), F32),
            small=vm((2, 2, 2, 2, 2, 16, 128), F32), small_c=vm((2, 2, 2, 2, 16, 128), F32), small_y=vm((2, 2, 2, 16, 128), F32),
            small_x=vm((2, 2, 16, 128), F32), small_zl=vm((2, 16, 128), F32), small_zh=vm((16, 128), F32),
        )
    scratch.update(
        local_sem=pltpu.SemaphoreType.DMA((32,)), send_sem=pltpu.SemaphoreType.DMA((72,)), recv_sem=pltpu.SemaphoreType.DMA((72,)),
    )
    names = [*ins, *outs, *scratch]
    results = pl.pallas_call(
        functools.partial(layer_kernel, names, rows, pad, fast),
        out_shape=tuple(outs.values()),
        in_specs=[spec for _, spec in ins.values()],
        out_specs=[in_vm] * len(outs),
        scratch_shapes=list(scratch.values()),
        compiler_params=pltpu.CompilerParams(collective_id=1, has_side_effects=True, vmem_limit_bytes=63 << 20),
        name="layer",
    )(*(value for value, _ in ins.values()))
    return dict(zip(outs, results))


def on_device(
    tokens, grad_out, freq_keep, lengths, first_gain, first_shift, qkv_weight, query_bias, value_bias, proj_weight,
    proj_bias, second_gain, second_shift, up_weight, up_bias, down_weight, down_bias,
):
    rows, width = tokens.shape[1:]
    clips = lax.axis_size("clip")
    freq = lax.axis_index("freq")
    fast = clips == 8
    attn, exps, queries, keys, values, out, inverse, first, gathered = attend(
        tokens, first_gain, first_shift, qkv_weight, query_bias, value_bias, freq_keep, lengths
    )
    got = layer_call(
        fast, tokens, grad_out, freq_keep, lengths,
        dict(
            first_gain=first_gain, proj_bias=proj_bias, second_gain=second_gain, second_shift=second_shift,
            up_bias=up_bias, down_bias=down_bias,
        ),
        dict(proj_hbm=proj_weight, up_hbm=up_weight, down_hbm=down_weight, qkv_hbm=qkv_weight),
        dict(
            attn_ref=attn, exp_hbm=exps, q_hbm=queries, k_hbm=keys, v_hbm=values, out_hbm=out, inv_hbm=inverse,
            first_hbm=first, tok_hbm=gathered,
        ),
    )
    rows_of = lambda padded: padded[None, :rows]
    if fast:
        small = got["small_fin"]
        piece = width // 32
        vectors = [small[row, :piece] for row in range(8)]
        quarter = lax.axis_index("clip") // 2
        up_bias_grad = lax.dynamic_index_in_dim(small[8:12], quarter, 0, keepdims=False)[: 4 * piece]
        mats = got["qkv_grad"], got["proj_grad"], got["up_grad"], got["down_grad"]
    else:
        half, core = width // 2, freq % 2

        def scatter(whole):
            return lax.psum_scatter(whole, ("clip", "freq"), scatter_dimension=0, tiled=True)

        def spread(part):
            placed = jnp.zeros((part.shape[0], 2, half), F32)
            placed = lax.dynamic_update_slice(placed, part.astype(F32)[:, None], (0, core, 0))
            return placed.reshape(part.shape[0], width)

        ups = got["g_up"].reshape(5, width, half)
        up = jnp.concatenate([spread(ups[chunk]) for chunk in range(4)], axis=1)
        start = (freq // 2) * 384 + (freq % 2) * 128
        qkv = jnp.concatenate(
            [
                lax.dynamic_update_slice(jnp.zeros((width, width), F32), part.astype(F32), (0, start))
                for part in got["g_qkv"].reshape(3, width, WIN)
            ],
            axis=1,
        )
        mats = scatter(qkv), scatter(spread(ups[4])), scatter(up), scatter(spread(got["g_down"].reshape(4 * width, half)))
        vectors = [scatter(got["vec"][row]) for row in range(8)]
        up_bias_grad = scatter(got["vec"][8:12].reshape(-1))
    qkv_grad, proj_grad, up_grad, down_grad = mats
    gain_one, shift_one, query, value, proj, gain_two, shift_two, down = vectors
    return (
        rows_of(got["block_out"]), rows_of(got["grad_tok"]), gain_one, shift_one, qkv_grad, query, value, proj_grad, proj,
        gain_two, shift_two, up_grad, up_bias_grad, down_grad, down,
    )


def solution(mesh):
    acts, both = P("clip", "freq", None), ("clip", "freq")
    mat, vec = P(both, None), P(both)
    return jax.shard_map(
        on_device,
        mesh=mesh,
        in_specs=(acts, acts, P("clip", None), P("clip")) + (P(),) * 13,
        out_specs=(acts, acts, vec, vec, mat, vec, vec, mat, vec, vec, vec, mat, vec, mat, vec),
        check_vma=False,
    )
```

```python
import functools
import types

import jax
import jax.numpy as jnp
from jax import lax
from jax.experimental import pallas as pl
from jax.experimental.pallas import tpu as pltpu
from jax.sharding import PartitionSpec as P

HEADS = 12
HEAD_DIM = 64
TIME_COLS = 99
EPS = 1e-06
F32 = jnp.float32
BF16 = jnp.bfloat16
MESH = pl.DeviceIdType.MESH
NT = (((1,), (1,)), ((), ()))
TN = (((0,), (0,)), ((), ()))
WIN = 256
GROUP = 4


def nt_dot(left, right):
    return lax.dot_general(left, right, NT, preferred_element_type=F32)


def tn_dot(left, right):
    return lax.dot_general(left, right, TN, preferred_element_type=F32)


def dot(left, right):
    return jnp.dot(left, right, preferred_element_type=F32)


def row_of(vector_ref):
    return vector_ref[...].reshape(1, -1)


def flip(index, stride):
    return index + stride - 2 * stride * ((index // stride) % 2)


def window_start(freq):
    return pl.multiple_of((freq // 2) * 384 + (freq % 2) * 128, 128)


def layer_stats(values):
    center = values - jnp.mean(values, -1, keepdims=True)
    inv_std = lax.rsqrt(jnp.mean(center * center, -1, keepdims=True) + EPS)
    return center * inv_std, inv_std


def head_lanes(core, head):
    lane = lax.broadcasted_iota(jnp.int32, (1, WIN), 1)
    first = 64 * core + 64 * head
    return (lane >= first) & (lane < first + 64)


def spare_lane(core, which):
    lane = lax.broadcasted_iota(jnp.int32, (1, WIN), 1)
    return lane == 192 * (1 - core) + which


def live_rows(shape, freq, keep_ref, length_ref, rows, first=0):
    slot = lax.broadcasted_iota(jnp.int32, shape, 0) + first
    live = jnp.zeros(shape, F32)
    per = rows // TIME_COLS
    for row in range(per):
        column = slot - row * TIME_COLS
        inside = (column >= 0) & (column < TIME_COLS) & (column < length_ref[0])
        kept = (keep_ref[0, freq * per + row] > 0).astype(F32)
        live = jnp.where(inside, kept, live)
    return live


DOWN_ORDER = ("xy", "xy", "xy", "yx")
UP_ORDER = ("lhxy", "yxlh", "lxyh", "lhyx", "xylh")
QKV_ORDER = ("xlh", "lxh", "lhx")
VECTORS = (
    "first_gain", "first_shift", "query_bias", "value_bias", "proj_bias", "second_gain", "second_shift", "up_bias", "down_bias",
)
HELD = (3,)
SCHEDULE = {
    "wp3": ("u0",),
    "t1": ("b3", "d0", "u1", "u2",),
    "gv": ("d1",),
    "t12": ("u0", "u3",),
    "gk": ("c0", "d2", "q2",),
    "tail": ("c1", "J0", "u1", "u2", "d3", "u0", "u4", "u3", "s", "q0", "q2", "c3", "c2", "J1", "u1", "Q2", "U0", "q1", "u2", "j0", "s", "u3", "q0", "U1", "q1", "U2", "u4", "s", "U3", "j1", "F", "Q0", "f", "s", "Q1", "u4", "U4", "G",),
}


class Transfers:
    def __init__(self, local_sem, send_sem, recv_sem):
        self.local_sem, self.send_sem, self.recv_sem = local_sem, send_sem, recv_sem
        self.locals, self.remotes = 0, 0

    def load(self, source, target):
        copy = pltpu.make_async_copy(source, target, self.local_sem.at[self.locals])
        self.locals += 1
        copy.start()
        return copy

    def send(self, source, target, device):
        copy = pltpu.make_async_remote_copy(
            src_ref=source, dst_ref=target, send_sem=self.send_sem.at[self.remotes],
            recv_sem=self.recv_sem.at[self.remotes], device_id=device, device_id_type=MESH,
        )
        self.remotes += 1
        copy.start()
        return copy


def lane_cut(ref, row, first, count):
    base, turn = first // 128 * 128, first % 128
    if turn + count <= 128:
        return pltpu.roll(ref[row : row + 8, base : base + 128], (128 - turn) % 128, 1)
    return pltpu.roll(ref[row : row + 8, base : base + 256], 256 - turn, 1)[:, 0:128]


def column_total(values):
    return jnp.sum(values, axis=0, keepdims=True)


def add_low(left, right):
    return (left.astype(F32) + right.astype(F32)).astype(BF16)


class Ladder:
    def __init__(self, transfers, places, whole, buffers):
        self.transfers, self.places, self.whole = transfers, places, whole
        self.buffers, self.step = buffers, 0

    def start(self):
        name, buffer = self.buffers[self.step]
        bit, partner = self.places[name]
        self.copy = self.transfers.send(self.whole.at[1 - bit], buffer, partner)

    def take(self, dtype):
        name, buffer = self.buffers[self.step]
        self.copy.wait()
        return (buffer[...].astype(F32) + self.whole[self.places[name][0]].astype(F32)).astype(dtype)

    def advance(self):
        buffer = self.buffers[self.step][1]
        buffer[...] = self.take(buffer.dtype)
        self.whole, self.step = buffer, self.step + 1
        if self.step < len(self.buffers):
            self.start()


def spread_rows(target, rows, axes, order):
    size = rows.shape[0] >> len(axes)
    for index in range(1 << len(axes)):
        bits = {name: (index >> (len(axes) - 1 - at)) & 1 for at, name in enumerate(axes)}
        target[tuple(bits[name] for name in order)] = rows[index * size : index * size + size]


def layer_kernel(names, rows, pad, fast, *refs):
    r = types.SimpleNamespace(**dict(zip(names, refs)))
    clip, freq = lax.axis_index("clip"), lax.axis_index("freq")
    core, side = freq % 2, freq // 2
    near, far, cross = flip(freq, 1), flip(freq, 2), flip(flip(freq, 1), 2)
    x_bit, z_low, z_high = clip % 2, (clip // 2) % 2, clip // 4
    to_near, to_far, to_cross = (clip, near), (clip, far), (clip, cross)
    to_x, to_zl, to_zh = (flip(clip, 1), freq), (flip(clip, 2), freq), (flip(clip, 4), freq)
    slots = GROUP * pad
    pair = 2 * pad
    half = 384
    t = Transfers(r.local_sem, r.send_sem, r.recv_sem)
    mine = pl.ds(pl.multiple_of(core * pad, 16), pad)
    my_half = pl.ds(pl.multiple_of(core * half, 128), half)
    near_half = pl.ds(pl.multiple_of((1 - core) * half, 128), half)
    start = window_start(freq)
    window = pl.ds(start, WIN)

    def load_down(chunk):
        return t.load(r.down_hbm.at[pl.ds(768 * (chunk % 4), 768), :], r.down_buf.at[chunk % 2])

    def load_up(chunk):
        return t.load(r.up_hbm.at[:, pl.ds(768 * chunk, 768)], r.up_buf.at[chunk % 2])

    vector_loads = [t.load(getattr(r, name + "_hbm"), getattr(r, name)) for name in VECTORS]
    load_wide = [
        t.load(r.qkv_hbm.at[:, pl.ds(pl.multiple_of(start + 768 * part, 128), WIN)], r.wide.at[:, pl.ds(WIN * part, WIN)])
        for part in range(3)
    ]
    partners = [to_near, to_far, to_cross] + ([to_x, to_zl, to_zh] if fast else [])
    barrier = pltpu.get_barrier_semaphore()
    for device in partners:
        pl.semaphore_signal(barrier, inc=1, device_id=device, device_id_type=MESH)
    r.tok[freq, pad - 16 : pad, :] = jnp.zeros((16, 768), BF16)
    r.tok[freq, 0:rows, :] = r.tok_ref[0]
    pl.semaphore_wait(barrier, len(partners))

    cuts = [(0, 80), (80, 80), (160, 80), (240, pad - 240)]
    far_copies = [
        t.send(r.tok.at[freq, pl.ds(first, count)], r.tok.at[freq, pl.ds(first, count)], to_far) for first, count in cuts
    ]
    near_copy = t.send(r.tok.at[freq], r.tok.at[freq], to_near)
    load_proj = t.load(r.proj_hbm, r.proj)
    down_loads = [load_down(0), load_down(1)]
    up_loads = [load_up(0), load_up(1)]

    def project(slot, first=0, count=pad):
        span = pl.ds(pl.multiple_of(slot * pad + first, 16), count)
        normed_one, _ = layer_stats(r.tok[slot, first : first + count].astype(F32))
        low = (normed_one * row_of(r.first_gain) + row_of(r.first_shift)).astype(BF16)
        r.first[span, :] = low
        live = live_rows((count, 1), slot, r.keep_ref, r.length_ref, rows, first)
        queries = (dot(low, r.wide[:, 0:WIN]) + r.query_bias[window].reshape(1, WIN)).astype(BF16).astype(F32) * 0.125
        keys = dot(low, r.wide[:, WIN : 2 * WIN])
        values = dot(low, r.wide[:, 2 * WIN : 3 * WIN]) + r.value_bias[window].reshape(1, WIN)
        one = spare_lane(core, 0)
        both = one | spare_lane(core, 1)
        r.q[span, :] = jnp.where(one, 1.0, queries).astype(BF16)
        r.k[span, :] = jnp.where(one, (live - 1.0) * 1e30, keys).astype(BF16)
        r.v[span, :] = jnp.where(both, 1.0, values).astype(BF16)

    for load in vector_loads + load_wide:
        load.wait()
    project(freq)
    near_copy.wait()
    project(near)
    keep = live_rows((pad, 1), freq, r.keep_ref, r.length_ref, rows)
    r.mid[pad - 16 : pad, :] = jnp.zeros((16, 768), F32)
    r.mid[0:rows, :] = r.tok_ref[0].astype(F32)
    r.grad[pad - 16 : pad, :] = jnp.zeros((16, 768), BF16)
    r.grad[0:rows, :] = r.grad_ref[0]
    r.grad[...] = (r.grad[...].astype(F32) * keep).astype(BF16)
    r.vec[...] = jnp.zeros_like(r.vec)
    r.dkt[...] = jnp.zeros_like(r.dkt)
    r.dvt[...] = jnp.zeros_like(r.dvt)
    r.grad2[mine, :] = r.grad[:, my_half]
    send_grad = t.send(r.grad.at[:, near_half], r.grad2.at[mine], to_near)
    for chunk in range(4):
        down_loads[chunk].wait()
        r.d_hidden[chunk] = nt_dot(r.grad[...], r.down_buf[chunk % 2]).astype(BF16)
        down_loads.append(load_down(chunk + 2))
    forwards = []

    def hand_on(part):
        first, count = cuts[part]
        far_copies[part].wait()
        forwards.append(t.send(r.tok.at[far, pl.ds(first, count)], r.tok.at[far, pl.ds(first, count)], to_near))

    hand_on(0)
    hand_on(1)
    project(far, 0, 160)
    forwards[0].wait()
    forwards[1].wait()
    hand_on(2)
    project(cross, 0, 160)
    hand_on(3)
    project(far, 160, pad - 160)
    forwards[2].wait()
    forwards[3].wait()
    project(cross, 160, pad - 160)

    out_sends, exp_saves, exp_loads = [], [], []
    for turn, slot in enumerate((far, cross, near, freq)):
        span = pl.ds(pl.multiple_of(slot * pad, 16), pad)
        stage = pl.ds(pl.multiple_of((slot % 2) * pad, 16), pad)
        q_rows = r.q[span, :]
        total = jnp.zeros((pad, WIN), F32)
        inverse = jnp.zeros((pad, 128), F32)
        for head in range(3):
            lanes = head_lanes(core, head)
            q_head = jnp.where(lanes | spare_lane(core, 0), q_rows, jnp.zeros_like(q_rows))
            scores = nt_dot(q_head, r.k[...])
            exps = jnp.exp(scores - jnp.max(scores, -1, keepdims=True)).astype(BF16)
            if turn >= 2:
                exp_saves[3 * (3 - turn) + head].wait()
            r.exps[head, stage, :] = exps
            if turn < 2:
                exp_saves.append(t.load(r.exps.at[head, stage], r.exp_hbm.at[head, stage]))
            mixed = dot(exps, r.v[...])
            scale = 1.0 / jnp.sum(jnp.where(spare_lane(core, 0), mixed, 0.0), -1, keepdims=True)
            total = jnp.where(lanes, mixed * scale, total)
            inverse = jnp.where(lax.broadcasted_iota(jnp.int32, (1, 128), 1) == head, scale, inverse)
        r.inv[span, :] = inverse
        r.out[span, :] = total.astype(BF16)
        if turn == 3:
            r.attn_in[freq] = total.astype(BF16)
        else:
            out_sends.append(t.send(r.out.at[span], r.attn_in.at[freq], (clip, slot)))
    for copy in out_sends:
        copy.wait()
    for side_in in range(2):
        left, right = r.attn_in[2 * side_in], r.attn_in[2 * side_in + 1]
        base = 384 * side_in
        r.att2[mine, base : base + 128] = left[:, 0:128]
        r.att2[mine, base + 128 : base + 256] = add_low(left[:, 128:256], right[:, 0:128])
        r.att2[mine, base + 256 : base + 384] = right[:, 128:256]
    send_att = t.send(r.att2.at[mine], r.att2.at[mine], to_near)

    load_proj.wait()
    middle = r.mid[...] + (dot(r.att2[mine, :], r.proj[...]) + row_of(r.proj_bias))
    r.mid[...] = middle
    normed, inv_two = layer_stats(middle)
    r.sec2[mine, :] = (normed * row_of(r.second_gain) + row_of(r.second_shift)).astype(BF16)
    send_sec = t.send(r.sec2.at[mine], r.sec2.at[mine], to_near)

    hid_sends, pre_sends = [None] * 4, [None] * 4

    def hid_rows(slot):
        return pl.ds(pl.multiple_of(slot * pair + core * pad, 16), pad)

    places = {"x": (x_bit, to_x), "y": (side, to_far), "l": (z_low, to_zl), "h": (z_high, to_zh), "c": (core, to_near)}
    downs, ups = [None] * 4, [None] * 5

    def start_up(chunk):
        if fast:
            ups[chunk] = Ladder(
                t, places, r.g_up.at[chunk],
                [(name, getattr(r, "up%d%s" % (chunk, name))) for name in UP_ORDER[chunk]],
            )
            ups[chunk].start()

    qkvs, smalls, joints, finals = [None] * 3, [], [None] * 2, []
    ended, late = [], {}

    def close_down(chunk):
        r.down_low[chunk // 2, chunk % 2] = downs[chunk].take(BF16)

    def progress(point):
        if not fast:
            return
        for step in SCHEDULE.get(point, ()):
            kind, index = step[0], int(step[1:] or 0)
            if kind == "u":
                ups[index].advance()
            elif kind == "d":
                downs[index].advance()
            elif kind == "q":
                qkvs[index].advance()
            elif kind == "s":
                smalls[0].advance()
            elif kind == "c":
                close_down(index)
            elif kind == "J":
                joints[index] = Ladder(t, places, r.down_low.at[index], [("l", r.down_l.at[index])])
                joints[index].start()
            elif kind == "j":
                joints[index].advance()
            elif kind == "F":
                finals.append(Ladder(t, places, r.down_l, [("h", r.down_h)]))
                finals[0].start()
            elif kind == "b":
                downs[index].start()
            elif kind == "U":
                total = ups[index].take(F32)
                r.up_fin[0, index] = total[0:24]
                r.up_fin[1, index] = total[24:48]
                ended.append(step)
                if sum(name[0] == "U" for name in ended) == 5:
                    late["up"] = t.send(r.up_fin.at[1 - core], r.up_c, to_near)
            elif kind == "Q":
                r.qkv_fin[:, :, WIN * index : WIN * index + WIN] = qkvs[index].take(F32).reshape(4, 24, WIN)
                ended.append(step)
                if sum(name[0] == "Q" for name in ended) == 3:
                    late["qkv"] = [
                        t.send(r.qkv_fin.at[other], r.qkv_c.at[freq], (clip, other)) for other in (far, cross, near)
                    ]
                    r.qkv_c[freq] = r.qkv_fin[freq]
            elif kind == "G":
                r.down_fin[...] = finals[0].take(F32).reshape(2, 96, half)
                late["down"] = t.send(r.down_fin.at[1 - core], r.down_c, to_near)
            elif kind == "f":
                first_norm_back()

    def weight_part(chunk):
        slot = chunk % 3
        g_down = tn_dot(r.hid2[pl.ds(slot * pair, pair), :], r.grad2[...]).astype(BF16)
        spread_rows(r.g_down.at[chunk // 2, chunk % 2], g_down, "xy", DOWN_ORDER[chunk] if fast else "xy")
        if fast:
            downs[chunk] = Ladder(
                t, places, r.g_down.at[chunk // 2, chunk % 2],
                [(name, getattr(r, "down%d%s" % (chunk, name))) for name in DOWN_ORDER[chunk]],
            )
            if chunk not in HELD:
                downs[chunk].start()
        g_up = tn_dot(r.sec2[...], r.pre2[slot]).astype(BF16)
        spread_rows(r.g_up.at[chunk], g_up, "hlxy", UP_ORDER[chunk] if fast else "hlxy")
        start_up(chunk)

    for chunk in range(4):
        slot = chunk % 3
        cut = slice(768 * chunk, 768 * chunk + 768)
        up_loads[chunk].wait()
        down_loads[4 + chunk].wait()
        up, down = r.up_buf[chunk % 2], r.down_buf[chunk % 2]
        inner = dot(r.sec2[mine, :], up) + r.up_bias[cut].reshape(1, 768)
        share = 0.5 * (1.0 + lax.erf(inner * 0.7071067811865476))
        hidden = (inner * share).astype(BF16)
        slope = share + inner * (0.3989422804014327 * jnp.exp(-0.5 * inner * inner))
        d_pre = (r.d_hidden[chunk].astype(F32) * slope).astype(BF16)
        r.hid2[hid_rows(slot), :] = hidden
        r.pre_out[chunk % 2] = d_pre
        r.pre2[slot, mine, :] = r.pre_out[chunk % 2, :, my_half]
        if chunk == 0:
            send_grad.wait()
            send_sec.wait()
        else:
            hid_sends[chunk - 1].wait()
            pre_sends[chunk - 1].wait()
        hid_sends[chunk] = t.send(r.hid2.at[hid_rows(slot)], r.hid2.at[hid_rows(slot)], to_near)
        pre_sends[chunk] = t.send(r.pre_out.at[chunk % 2, :, near_half], r.pre2.at[slot, mine], to_near)
        if chunk:
            weight_part(chunk - 1)
            progress("c%d" % chunk)
        r.vec[8 + chunk : 9 + chunk, :] = column_total(d_pre.astype(F32))
        more = dot(hidden, down)
        back = nt_dot(d_pre, up)
        if chunk == 0:
            r.ff[...] = more
            r.dsec[...] = back
        else:
            r.ff[...] += more
            r.dsec[...] += back
        if chunk + 2 < 4:
            up_loads.append(load_up(chunk + 2))
            down_loads.append(load_down(chunk + 6))

    d_second = r.dsec[...]
    normed, inv_two = layer_stats(r.mid[...])
    r.vec[5:6, :] = column_total(d_second * normed)
    r.vec[6:7, :] = column_total(d_second)
    scaled = d_second * row_of(r.second_gain)
    grad_rows = r.grad[...].astype(F32)
    r.vec[7:8, :] = column_total(grad_rows)
    d_mid = grad_rows + inv_two * (
        scaled
        - jnp.mean(scaled, -1, keepdims=True)
        - normed * jnp.mean(scaled * normed, -1, keepdims=True)
    )
    r.dsec[...] = d_mid
    branch = d_mid.astype(BF16)
    r.vec[4:5, :] = column_total(branch.astype(F32))
    r.branch[...] = branch
    r.dattn[...] = nt_dot(branch, r.proj[...]).astype(BF16)
    attn_sends = [
        t.send(r.dattn.at[:, pl.ds(window_start(other), WIN)], r.dout.at[freq], (clip, other))
        for other in (far, cross, near)
    ]
    r.branch2[mine, :] = r.branch[:, my_half]
    send_branch = t.send(r.branch.at[:, near_half], r.branch2.at[mine], to_near)
    r.dout[freq] = r.dattn[:, window]
    r.grad[...] = (keep * (r.mid[...] + (r.ff[...] + row_of(r.down_bias)))).astype(BF16)
    stores = [t.load(r.grad, r.block_out_hbm)]
    hid_sends[3].wait()
    pre_sends[3].wait()
    weight_part(3)
    progress("wp3")
    send_att.wait()
    send_branch.wait()
    g_proj = tn_dot(r.att2[...], r.branch2[...]).astype(BF16)
    spread_rows(r.g_up.at[4], g_proj, "hlxy", UP_ORDER[4] if fast else "hlxy")
    start_up(4)
    progress("gproj")

    def qkv_part(part):
        g_qkv = tn_dot(r.first[...], r.hid2[0:slots, WIN * part : WIN * part + WIN]).astype(BF16)
        spread_rows(r.g_qkv.at[part], g_qkv, "hlx", QKV_ORDER[part] if fast else "hlx")
        if fast:
            qkvs[part] = Ladder(
                t, places, r.g_qkv.at[part], [(name, getattr(r, "qkv%d%s" % (part, name))) for name in QKV_ORDER[part]]
            )
            qkvs[part].start()

    def finish(small):
        late["up"].wait()
        for chunk in range(5):
            place = r.up_grad if chunk < 4 else r.proj_grad
            base = 768 * (chunk % 4)
            place[:, pl.ds(pl.multiple_of(base + half * core, 128), half)] = r.up_fin[core, chunk]
            place[:, pl.ds(pl.multiple_of(base + half * (1 - core), 128), half)] = r.up_c[chunk]
        stores.append(t.load(r.up_grad, r.up_grad_hbm))
        stores.append(t.load(r.proj_grad, r.proj_grad_hbm))
        for copy in late["qkv"]:
            copy.wait()
        for part in range(3):
            for other in range(2):
                left = r.qkv_c[2 * other, :, WIN * part : WIN * part + WIN]
                right = r.qkv_c[2 * other + 1, :, WIN * part : WIN * part + WIN]
                base = 768 * part + 384 * other
                r.qkv_grad[:, base : base + 128] = left[:, 0:128]
                r.qkv_grad[:, base + 128 : base + 256] = left[:, 128:256] + right[:, 0:128]
                r.qkv_grad[:, base + 256 : base + 384] = right[:, 128:256]
        stores.append(t.load(r.qkv_grad, r.qkv_grad_hbm))
        r.small_fin[...] = small.take(F32)
        stores.append(t.load(r.small_fin, r.small_fin_hbm))
        late["down"].wait()
        r.down_grad[:, my_half] = r.down_fin[core]
        r.down_grad[:, near_half] = r.down_c[...]
        stores.append(t.load(r.down_grad, r.down_grad_hbm))

    blocks = (side, 1 - side)
    head_rows = [pl.ds(pl.multiple_of(64 * core + 64 * head, 64), 64) for head in range(3)]
    for turn in range(2):
        block = blocks[turn]
        at = pl.ds(pl.multiple_of(block * pair, 16), pair)
        if turn == 0:
            attn_sends[2].wait()
        else:
            attn_sends[0].wait()
            attn_sends[1].wait()
            progress("t1")
        grads = jnp.concatenate([r.dout[2 * block].astype(F32), r.dout[2 * block + 1].astype(F32)], axis=0)
        scales = jnp.zeros((pair, WIN), F32)
        for head in range(3):
            scales = jnp.where(head_lanes(core, head), r.inv[at, head : head + 1], scales)
        grads = grads * scales
        r.dscaled[...] = grads.astype(BF16)
        r.qt[...] = r.q[at, :].astype(F32).T.astype(BF16)
        r.dot_t[...] = grads.T.astype(BF16)
        products = grads * r.out[at, :].astype(F32)
        dq_total = jnp.zeros((pair, WIN), F32)

        def value_part(head):
            if turn == 1:
                exp_loads[head].wait()
            r.dvt[head_rows[head], :] += dot(r.dot_t[head_rows[head], :], r.exps[head])

        if turn == 1:
            for head in range(3):
                value_part(head)
            r.hid2[0:slots, 2 * WIN : 3 * WIN] = r.dvt[...].T.astype(BF16)
            qkv_part(2)
            progress("gv")
        for head in range(3):
            lanes = head_lanes(core, head)
            mean = jnp.sum(jnp.where(lanes, products, 0.0), -1, keepdims=True)
            high = mean.astype(BF16).astype(F32)
            fill = jnp.where(spare_lane(core, 0), -high, jnp.where(spare_lane(core, 1), high - mean, 0.0))
            d_head = jnp.where(lanes, r.dscaled[...].astype(F32), fill).astype(BF16)
            if turn == 0:
                value_part(head)
            d_prob = nt_dot(d_head, r.v[...])
            d_score = (r.exps[head].astype(F32) * d_prob).astype(BF16)
            dq_total = jnp.where(lanes, dot(d_score, r.k[...]), dq_total)
            r.dkt[head_rows[head], :] += dot(r.qt[head_rows[head], :], d_score)
            if turn == 0:
                exp_loads.append(t.load(r.exp_hbm.at[head], r.exps.at[head]))
        r.hid2[at, 0:WIN] = (dq_total * 0.125).astype(BF16)
        if turn == 1:
            progress("t12")
    r.hid2[0:slots, WIN : 2 * WIN] = r.dkt[...].T.astype(BF16)
    r.vec[2:3, window] = column_total(r.hid2[0:slots, 0:WIN].astype(F32))
    r.vec[3:4, window] = column_total(r.hid2[0:slots, 2 * WIN : 3 * WIN].astype(F32))

    def first_back(slot):
        at = pl.ds(pl.multiple_of(slot * pad, 16), pad)
        d_first = nt_dot(r.hid2[at, :], r.wide[...])
        normed_one, inv_one = layer_stats(r.tok[slot].astype(F32))
        r.vec[0:1, :] += column_total(d_first * normed_one)
        r.vec[1:2, :] += column_total(d_first)
        return d_first, normed_one, inv_one

    r.sec2[0:pad, :] = first_back(cross)[0].astype(BF16)
    send_cross = t.send(r.sec2.at[pl.ds(0, pad)], r.first_near.at[0], to_near)
    r.branch[...] = first_back(far)[0].astype(BF16)
    progress("fb")
    send_cross.wait()
    r.branch[...] = add_low(r.branch[...], r.first_near[0])
    send_far = t.send(r.branch, r.first_far, to_far)
    qkv_part(1)
    progress("gk")
    qkv_part(0)
    progress("gq")
    r.sec2[pad:pair, :] = first_back(near)[0].astype(BF16)
    send_first = t.send(r.sec2.at[pl.ds(pad, pad)], r.first_near.at[1], to_near)
    own_first, normed_one, inv_one = first_back(freq)
    r.ff[...] = own_first

    def first_norm_back():
        send_first.wait()
        send_far.wait()
        d_first = r.ff[...] + r.first_near[1].astype(F32) + r.first_far[...].astype(F32)
        scaled = d_first * row_of(r.first_gain)
        r.dattn[...] = (
            r.dsec[...]
            + inv_one
            * (
                scaled
                - jnp.mean(scaled, -1, keepdims=True)
                - normed_one * jnp.mean(scaled * normed_one, -1, keepdims=True)
            )
        ).astype(BF16)
        stores.append(t.load(r.dattn, r.grad_tok_hbm))

    if fast:
        biases = [lane_cut(r.vec, 8, 96 * index, 96) for index in range(8)]
        for index in range(32):
            at = tuple((index >> bit) & 1 for bit in range(5))
            r.small[at + (slice(0, 8), slice(None))] = lane_cut(r.vec, 0, 24 * index, 24)
            r.small[at + (slice(8, 16), slice(None))] = biases[index % 8]
        small = Ladder(t, places, r.small, [(name, getattr(r, "small_" + name)) for name in "cyxlh"])
        small.start()
        smalls.append(small)
        progress("tail")
    else:
        first_norm_back()
    if fast:
        finish(small)
    for store in stores:
        store.wait()


def layer_call(fast, tokens, grad_out, keep, lengths, vectors, weights):
    rows, width = tokens.shape[1:]
    pad = -(-rows // 16) * 16
    slots, pair, half = GROUP * pad, 2 * pad, width // 2
    wide = 4 * width
    sd, vm = jax.ShapeDtypeStruct, pltpu.VMEM
    in_vm, in_sm, in_hbm = pl.BlockSpec(memory_space=pltpu.VMEM), pl.BlockSpec(memory_space=pltpu.SMEM), pl.BlockSpec(memory_space=pl.ANY)
    ins = {
        "tok_ref": (tokens, in_vm), "grad_ref": (grad_out, in_vm), "keep_ref": (keep, in_sm), "length_ref": (lengths, in_sm),
    }
    for name, value in vectors.items():
        ins[name + "_hbm"] = (value, in_hbm)
    for name, value in weights.items():
        ins[name] = (value, in_hbm)
    outs = {"block_out_hbm": sd((pad, width), BF16), "grad_tok_hbm": sd((pad, width), BF16), "exp_hbm": sd((3, pair, slots), BF16)}
    if fast:
        outs.update(
            qkv_grad_hbm=sd((24, 3 * width), F32), proj_grad_hbm=sd((24, width), F32), up_grad_hbm=sd((24, wide), F32),
            down_grad_hbm=sd((96, width), F32), small_fin_hbm=sd((16, 128), F32),
        )
    else:
        outs.update(
            g_qkv=sd((3, 2, 2, 2, 96, WIN), BF16), g_up=sd((5, 2, 2, 2, 2, 48, half), BF16),
            g_down=sd((2, 2, 2, 2, 192, half), BF16), vec=sd((16, width), F32),
        )
    scratch = {
        "proj": vm((width, width), BF16), "up_buf": vm((2, width, width), BF16), "down_buf": vm((2, width, width), BF16),
        "q": vm((slots, WIN), BF16), "k": vm((slots, WIN), BF16), "v": vm((slots, WIN), BF16),
        "inv": vm((slots, 128), F32), "out": vm((slots, WIN), BF16), "attn_in": vm((GROUP, pad, WIN), BF16), "wide": vm((width, 3 * WIN), BF16), "first": vm((slots, width), BF16),
        "tok": vm((GROUP, pad, width), BF16),
        "mid": vm((pad, width), F32), "grad": vm((pad, width), BF16), "d_hidden": vm((4, pad, width), BF16),
        "ff": vm((pad, width), F32), "dsec": vm((pad, width), F32),
        "grad2": vm((pair, half), BF16), "att2": vm((pair, width), BF16), "sec2": vm((pair, width), BF16),
        "hid2": vm((3 * pair, width), BF16), "pre2": vm((3, pair, half), BF16), "pre_out": vm((2, pad, width), BF16),
        "branch": vm((pad, width), BF16), "branch2": vm((pair, half), BF16), "dattn": vm((pad, width), BF16),
        "dout": vm((GROUP, pad, WIN), BF16), "dscaled": vm((pair, WIN), BF16), "qt": vm((WIN, pair), BF16),
        "dot_t": vm((WIN, pair), BF16), "exps": vm((3, pair, slots), BF16), "dkt": vm((WIN, slots), F32),
        "dvt": vm((WIN, slots), F32),
        "first_near": vm((2, pad, width), BF16), "first_far": vm((pad, width), BF16),
    }
    for name, value in vectors.items():
        scratch[name] = vm(value.shape, F32)
    for name, value in outs.items():
        if name not in ("block_out_hbm", "grad_tok_hbm", "exp_hbm") and name.endswith("_hbm"):
            scratch[name[:-4]] = vm(value.shape, value.dtype)
    if fast:
        scratch.update(
            vec=vm((16, width), F32),
            g_down=vm((2, 2, 2, 2, 192, half), BF16), down_low=vm((2, 2, 192, half), BF16),
            down_l=vm((2, 192, half), BF16), down_h=vm((192, half), BF16), down_fin=vm((2, 96, half), F32), down_c=vm((96, half), F32),
            g_up=vm((5, 2, 2, 2, 2, 48, half), BF16), up_fin=vm((2, 5, 24, half), F32), up_c=vm((5, 24, half), F32),
            g_qkv=vm((3, 2, 2, 2, 96, WIN), BF16), qkv_fin=vm((4, 24, 3 * WIN), F32), qkv_c=vm((4, 24, 3 * WIN), F32),
            small=vm((2, 2, 2, 2, 2, 16, 128), F32), small_h=vm((16, 128), F32),
        )
        for chunk, order in enumerate(DOWN_ORDER):
            for step, name in enumerate(order):
                scratch["down%d%s" % (chunk, name)] = vm((2,) * (1 - step) + (192, half), BF16)
        for step, name in enumerate("cyxl"):
            scratch["small_" + name] = vm((2,) * (4 - step) + (16, 128), F32)
        for chunk, order in enumerate(UP_ORDER):
            for step, name in enumerate(order):
                scratch["up%d%s" % (chunk, name)] = vm((2,) * (3 - step) + (48, half), BF16)
        for part, order in enumerate(QKV_ORDER):
            for step, name in enumerate(order):
                scratch["qkv%d%s" % (part, name)] = vm((2,) * (2 - step) + (96, WIN), BF16)
    scratch.update(
        local_sem=pltpu.SemaphoreType.DMA((56,)), send_sem=pltpu.SemaphoreType.DMA((96,)), recv_sem=pltpu.SemaphoreType.DMA((96,)),
    )
    names = [*ins, *outs, *scratch]
    results = pl.pallas_call(
        functools.partial(layer_kernel, names, rows, pad, fast),
        out_shape=tuple(outs.values()),
        in_specs=[spec for _, spec in ins.values()],
        out_specs=[in_hbm if name.endswith("_hbm") else in_vm for name in outs],
        scratch_shapes=list(scratch.values()),
        compiler_params=pltpu.CompilerParams(collective_id=0, has_side_effects=True, vmem_limit_bytes=63 << 20),
        name="layer",
    )(*(value for value, _ in ins.values()))
    return {name.removesuffix("_hbm"): result for name, result in zip(outs, results)}


def close_kernel(rows, *refs):
    count = 6
    for index, (source, target) in enumerate(zip(refs[:count], refs[count + 1 :])):
        if index < 2:
            target[0] = source[0:rows, :]
        else:
            target[...] = source[...]
    small, vectors = refs[count], refs[2 * count + 1 :]
    for row, vector in enumerate(vectors[:8]):
        vector[...] = small[row, 0 : vector.shape[0]]
    quarter = lax.axis_index("clip") // 2
    biases = small[8, :]
    for index in range(1, 4):
        biases = jnp.where(quarter == index, small[8 + index, :], biases)
    vectors[8][...] = biases[0 : vectors[8].shape[0]]


def close(rows, arrays, small):
    shapes = [(1, rows, array.shape[1]) if index < 2 else array.shape for index, array in enumerate(arrays)]
    piece = arrays[0].shape[1] // 32
    outs = [jax.ShapeDtypeStruct(shape, array.dtype) for shape, array in zip(shapes, arrays)]
    outs += [jax.ShapeDtypeStruct((size,), F32) for size in [piece] * 8 + [4 * piece]]
    spec = pl.BlockSpec(memory_space=pltpu.VMEM)
    return pl.pallas_call(
        functools.partial(close_kernel, rows),
        out_shape=tuple(outs),
        in_specs=[spec] * (len(arrays) + 1),
        out_specs=[spec] * len(outs),
        name="close",
    )(*arrays, small)


def on_device(
    tokens, grad_out, freq_keep, lengths, first_gain, first_shift, qkv_weight, query_bias, value_bias, proj_weight,
    proj_bias, second_gain, second_shift, up_weight, up_bias, down_weight, down_bias,
):
    rows, width = tokens.shape[1:]
    clips = lax.axis_size("clip")
    freq = lax.axis_index("freq")
    fast = clips == 8
    got = layer_call(
        fast, tokens, grad_out, freq_keep, lengths,
        dict(
            first_gain=first_gain, first_shift=first_shift, query_bias=query_bias, value_bias=value_bias, proj_bias=proj_bias, second_gain=second_gain, second_shift=second_shift,
            up_bias=up_bias, down_bias=down_bias,
        ),
        dict(proj_hbm=proj_weight, up_hbm=up_weight, down_hbm=down_weight, qkv_hbm=qkv_weight),
    )
    if fast:
        names = ("block_out", "grad_tok", "qkv_grad", "proj_grad", "up_grad", "down_grad")
        results = close(rows, [got[name] for name in names], got["small_fin"])
        block_out, grad_tok, mats, vectors, up_bias_grad = results[0], results[1], results[2:6], results[6:14], results[14]
    else:
        half, core = width // 2, freq % 2
        block_out, grad_tok = got["block_out"][None, :rows], got["grad_tok"][None, :rows]

        def scatter(whole):
            return lax.psum_scatter(whole, ("clip", "freq"), scatter_dimension=0, tiled=True)

        def spread(part):
            placed = jnp.zeros((part.shape[0], 2, half), F32)
            placed = lax.dynamic_update_slice(placed, part.astype(F32)[:, None], (0, core, 0))
            return placed.reshape(part.shape[0], width)

        ups = got["g_up"].reshape(5, width, half)
        up = jnp.concatenate([spread(ups[chunk]) for chunk in range(4)], axis=1)
        start = (freq // 2) * 384 + (freq % 2) * 128
        qkv = jnp.concatenate(
            [
                lax.dynamic_update_slice(jnp.zeros((width, width), F32), part.astype(F32), (0, start))
                for part in got["g_qkv"].reshape(3, width, WIN)
            ],
            axis=1,
        )
        mats = scatter(qkv), scatter(spread(ups[4])), scatter(up), scatter(spread(got["g_down"].reshape(4 * width, half)))
        vectors = [scatter(got["vec"][row]) for row in range(8)]
        up_bias_grad = scatter(got["vec"][8:12].reshape(-1))
    qkv_grad, proj_grad, up_grad, down_grad = mats
    gain_one, shift_one, query, value, proj, gain_two, shift_two, down = vectors
    return (
        block_out, grad_tok, gain_one, shift_one, qkv_grad, query, value, proj_grad, proj,
        gain_two, shift_two, up_grad, up_bias_grad, down_grad, down,
    )


def solution(mesh):
    acts, both = P("clip", "freq", None), ("clip", "freq")
    mat, vec = P(both, None), P(both)
    return jax.shard_map(
        on_device,
        mesh=mesh,
        in_specs=(acts, acts, P("clip", None), P("clip")) + (P(),) * 13,
        out_specs=(acts, acts, vec, vec, mat, vec, vec, mat, vec, vec, vec, mat, vec, mat, vec),
        check_vma=False,
    )
```

```python
import functools
import types

import jax
import jax.numpy as jnp
from jax import lax
from jax.experimental import pallas as pl
from jax.experimental.pallas import tpu as pltpu
from jax.sharding import PartitionSpec as P

HEADS = 12
HEAD_DIM = 64
TIME_COLS = 99
EPS = 1e-06
F32 = jnp.float32
BF16 = jnp.bfloat16
MESH = pl.DeviceIdType.MESH
NT = (((1,), (1,)), ((), ()))
TN = (((0,), (0,)), ((), ()))
WIN = 256
GROUP = 4


def nt_dot(left, right):
    return lax.dot_general(left, right, NT, preferred_element_type=F32)


def tn_dot(left, right):
    return lax.dot_general(left, right, TN, preferred_element_type=F32)


def dot(left, right):
    return jnp.dot(left, right, preferred_element_type=F32)


def row_of(vector_ref):
    return vector_ref[...].reshape(1, -1)


def flip(index, stride):
    return index + stride - 2 * stride * ((index // stride) % 2)


def window_start(freq):
    return pl.multiple_of((freq // 2) * 384 + (freq % 2) * 128, 128)


def layer_stats(values):
    center = values - jnp.mean(values, -1, keepdims=True)
    inv_std = lax.rsqrt(jnp.mean(center * center, -1, keepdims=True) + EPS)
    return center * inv_std, inv_std


def head_lanes(core, head):
    lane = lax.broadcasted_iota(jnp.int32, (1, WIN), 1)
    first = 64 * core + 64 * head
    return (lane >= first) & (lane < first + 64)


def spare_lane(core, which):
    lane = lax.broadcasted_iota(jnp.int32, (1, WIN), 1)
    return lane == 192 * (1 - core) + which


def live_rows(shape, freq, keep_ref, length_ref, rows, first=0):
    slot = lax.broadcasted_iota(jnp.int32, shape, 0) + first
    live = jnp.zeros(shape, F32)
    per = rows // TIME_COLS
    for row in range(per):
        column = slot - row * TIME_COLS
        inside = (column >= 0) & (column < TIME_COLS) & (column < length_ref[0])
        kept = (keep_ref[0, freq * per + row] > 0).astype(F32)
        live = jnp.where(inside, kept, live)
    return live


DOWN_ORDER = ("xy", "yx", "xy", "yx")
UP_ORDER = ("lhxy", "xylh", "lxyh", "xylh", "lhxy")
QKV_ORDER = ("xlh", "lxh", "lhx")
VECTORS = (
    "first_gain", "first_shift", "query_bias", "value_bias", "proj_bias", "second_gain", "second_shift", "up_bias", "down_bias",
)
PACKED = ((slice(256, 384), slice(256, 384)), (slice(0, 256), slice(0, 256)), (slice(0, 256), slice(384, 640)))
HELD = (3,)
SCHEDULE = {
    "wp3": ("u0",),
    "t1": ("b3", "d0", "d1", "u2",),
    "gv": ("u0",),
    "t12": ("u1", "u4",),
    "gk": ("c0", "d2", "q2",),
    "tail": ("d3", "u0", "u1", "c1", "J0", "u2", "u4", "u3", "s", "q0", "q2", "U0", "u4", "c3", "Q2", "c2", "J1", "u1", "q0", "q1", "j0", "u2", "s", "U4", "Q0", "q1", "U1", "s", "u3", "U2", "j1", "F", "s", "Q1", "f", "u3", "U3", "G",),
}


class Transfers:
    def __init__(self, local_sem, send_sem, recv_sem):
        self.local_sem, self.send_sem, self.recv_sem = local_sem, send_sem, recv_sem
        self.locals, self.remotes = 0, 0

    def load(self, source, target):
        copy = pltpu.make_async_copy(source, target, self.local_sem.at[self.locals])
        self.locals += 1
        copy.start()
        return copy

    def send(self, source, target, device):
        copy = pltpu.make_async_remote_copy(
            src_ref=source, dst_ref=target, send_sem=self.send_sem.at[self.remotes],
            recv_sem=self.recv_sem.at[self.remotes], device_id=device, device_id_type=MESH,
        )
        self.remotes += 1
        copy.start()
        return copy


def lane_cut(ref, row, first, count):
    base, turn = first // 128 * 128, first % 128
    if turn + count <= 128:
        return pltpu.roll(ref[row : row + 8, base : base + 128], (128 - turn) % 128, 1)
    return pltpu.roll(ref[row : row + 8, base : base + 256], 256 - turn, 1)[:, 0:128]


def column_total(values):
    return jnp.sum(values, axis=0, keepdims=True)


def add_low(left, right):
    return (left.astype(F32) + right.astype(F32)).astype(BF16)


class Ladder:
    def __init__(self, transfers, places, whole, buffers):
        self.transfers, self.places, self.whole = transfers, places, whole
        self.buffers, self.step = buffers, 0

    def start(self):
        name, buffer = self.buffers[self.step]
        bit, partner = self.places[name]
        self.copy = self.transfers.send(self.whole.at[1 - bit], buffer, partner)

    def take(self, dtype):
        name, buffer = self.buffers[self.step]
        self.copy.wait()
        return (buffer[...].astype(F32) + self.whole[self.places[name][0]].astype(F32)).astype(dtype)

    def advance(self):
        buffer = self.buffers[self.step][1]
        buffer[...] = self.take(buffer.dtype)
        self.whole, self.step = buffer, self.step + 1
        if self.step < len(self.buffers):
            self.start()


def spread_rows(target, rows, axes, order):
    size = rows.shape[0] >> len(axes)
    for index in range(1 << len(axes)):
        bits = {name: (index >> (len(axes) - 1 - at)) & 1 for at, name in enumerate(axes)}
        target[tuple(bits[name] for name in order)] = rows[index * size : index * size + size]


def layer_kernel(names, rows, pad, fast, *refs):
    r = types.SimpleNamespace(**dict(zip(names, refs)))
    clip, freq = lax.axis_index("clip"), lax.axis_index("freq")
    core, side = freq % 2, freq // 2
    near, far, cross = flip(freq, 1), flip(freq, 2), flip(flip(freq, 1), 2)
    x_bit, z_low, z_high = clip % 2, (clip // 2) % 2, clip // 4
    to_near, to_far, to_cross = (clip, near), (clip, far), (clip, cross)
    to_x, to_zl, to_zh = (flip(clip, 1), freq), (flip(clip, 2), freq), (flip(clip, 4), freq)
    slots = GROUP * pad
    pair = 2 * pad
    half = 384
    t = Transfers(r.local_sem, r.send_sem, r.recv_sem)
    mine = pl.ds(pl.multiple_of(core * pad, 16), pad)
    my_half = pl.ds(pl.multiple_of(core * half, 128), half)
    near_half = pl.ds(pl.multiple_of((1 - core) * half, 128), half)
    start = window_start(freq)
    window = pl.ds(start, WIN)

    def load_down(chunk):
        return t.load(r.down_hbm.at[pl.ds(768 * (chunk % 4), 768), :], r.down_buf.at[chunk % 2])

    def load_up(chunk):
        return t.load(r.up_hbm.at[:, pl.ds(768 * chunk, 768)], r.up_buf.at[chunk % 2])

    vector_loads = [t.load(getattr(r, name + "_hbm"), getattr(r, name)) for name in VECTORS]
    load_wide = [
        t.load(r.qkv_hbm.at[:, pl.ds(pl.multiple_of(start + 768 * part, 128), WIN)], r.wide.at[:, pl.ds(WIN * part, WIN)])
        for part in range(3)
    ]
    partners = [to_near, to_far, to_cross] + ([to_x, to_zl, to_zh] if fast else [])
    barrier = pltpu.get_barrier_semaphore()
    for device in partners:
        pl.semaphore_signal(barrier, inc=1, device_id=device, device_id_type=MESH)
    r.tok[freq, pad - 16 : pad, :] = jnp.zeros((16, 768), BF16)
    r.tok[freq, 0:rows, :] = r.tok_ref[0]
    pl.semaphore_wait(barrier, len(partners))

    cuts = [(0, 80), (80, 80), (160, 80), (240, pad - 240)]
    far_copies = [
        t.send(r.tok.at[freq, pl.ds(first, count)], r.tok.at[freq, pl.ds(first, count)], to_far) for first, count in cuts
    ]
    near_copy = t.send(r.tok.at[freq], r.tok.at[freq], to_near)
    load_proj = t.load(r.proj_hbm, r.proj)
    down_loads = [load_down(0), load_down(1)]
    up_loads = [load_up(0), load_up(1)]

    def project(slot, first=0, count=pad):
        span = pl.ds(pl.multiple_of(slot * pad + first, 16), count)
        normed_one, _ = layer_stats(r.tok[slot, first : first + count].astype(F32))
        low = (normed_one * row_of(r.first_gain) + row_of(r.first_shift)).astype(BF16)
        r.first[span, :] = low
        live = live_rows((count, 1), slot, r.keep_ref, r.length_ref, rows, first)
        queries = (dot(low, r.wide[:, 0:WIN]) + r.query_bias[window].reshape(1, WIN)).astype(BF16).astype(F32) * 0.125
        keys = dot(low, r.wide[:, WIN : 2 * WIN])
        values = dot(low, r.wide[:, 2 * WIN : 3 * WIN]) + r.value_bias[window].reshape(1, WIN)
        one = spare_lane(core, 0)
        both = one | spare_lane(core, 1)
        r.q[span, :] = jnp.where(one, 1.0, queries).astype(BF16)
        r.k[span, :] = jnp.where(one, (live - 1.0) * 1e30, keys).astype(BF16)
        r.v[span, :] = jnp.where(both, 1.0, values).astype(BF16)

    for load in vector_loads + load_wide:
        load.wait()
    project(freq)
    near_copy.wait()
    project(near)
    keep = live_rows((pad, 1), freq, r.keep_ref, r.length_ref, rows)
    r.mid[pad - 16 : pad, :] = jnp.zeros((16, 768), F32)
    r.mid[0:rows, :] = r.tok_ref[0].astype(F32)
    r.grad[pad - 16 : pad, :] = jnp.zeros((16, 768), BF16)
    r.grad[0:rows, :] = r.grad_ref[0]
    r.grad[...] = (r.grad[...].astype(F32) * keep).astype(BF16)
    r.vec[...] = jnp.zeros_like(r.vec)
    r.dkt[...] = jnp.zeros_like(r.dkt)
    r.dvt[...] = jnp.zeros_like(r.dvt)
    r.grad2[mine, :] = r.grad[:, my_half]
    send_grad = t.send(r.grad.at[:, near_half], r.grad2.at[mine], to_near)
    for chunk in range(4):
        down_loads[chunk].wait()
        r.d_hidden[chunk] = nt_dot(r.grad[...], r.down_buf[chunk % 2]).astype(BF16)
        down_loads.append(load_down(chunk + 2))
    forwards = []

    def hand_on(part):
        first, count = cuts[part]
        far_copies[part].wait()
        forwards.append(t.send(r.tok.at[far, pl.ds(first, count)], r.tok.at[far, pl.ds(first, count)], to_near))

    hand_on(0)
    hand_on(1)
    project(far, 0, 160)
    forwards[0].wait()
    forwards[1].wait()
    hand_on(2)
    project(cross, 0, 160)
    hand_on(3)
    project(far, 160, pad - 160)
    forwards[2].wait()
    forwards[3].wait()
    project(cross, 160, pad - 160)

    out_sends, exp_saves, exp_loads = [], [], []
    for turn, slot in enumerate((far, cross, near, freq)):
        span = pl.ds(pl.multiple_of(slot * pad, 16), pad)
        stage = pl.ds(pl.multiple_of((slot % 2) * pad, 16), pad)
        q_rows = r.q[span, :]
        total = jnp.zeros((pad, WIN), F32)
        inverse = jnp.zeros((pad, 128), F32)
        for head in range(3):
            lanes = head_lanes(core, head)
            q_head = jnp.where(lanes | spare_lane(core, 0), q_rows, jnp.zeros_like(q_rows))
            scores = nt_dot(q_head, r.k[...])
            exps = jnp.exp(scores - jnp.max(scores, -1, keepdims=True)).astype(BF16)
            if turn >= 2:
                exp_saves[3 * (3 - turn) + head].wait()
            r.exps[head, stage, :] = exps
            if turn < 2:
                exp_saves.append(t.load(r.exps.at[head, stage], r.exp_hbm.at[head, stage]))
            mixed = dot(exps, r.v[...])
            scale = 1.0 / jnp.sum(jnp.where(spare_lane(core, 0), mixed, 0.0), -1, keepdims=True)
            total = jnp.where(lanes, mixed * scale, total)
            inverse = jnp.where(lax.broadcasted_iota(jnp.int32, (1, 128), 1) == head, scale, inverse)
        r.inv[span, :] = inverse
        r.out[span, :] = total.astype(BF16)
        if turn == 3:
            r.attn_in[freq] = total.astype(BF16)
        else:
            out_sends.append(t.send(r.out.at[span], r.attn_in.at[freq], (clip, slot)))
    for copy in out_sends:
        copy.wait()
    for side_in in range(2):
        left, right = r.attn_in[2 * side_in], r.attn_in[2 * side_in + 1]
        base = 384 * side_in
        r.att2[mine, base : base + 128] = left[:, 0:128]
        r.att2[mine, base + 128 : base + 256] = add_low(left[:, 128:256], right[:, 0:128])
        r.att2[mine, base + 256 : base + 384] = right[:, 128:256]
    send_att = t.send(r.att2.at[mine], r.att2.at[mine], to_near)

    load_proj.wait()
    middle = r.mid[...] + (dot(r.att2[mine, :], r.proj[...]) + row_of(r.proj_bias))
    r.mid[...] = middle
    normed, inv_two = layer_stats(middle)
    r.sec2[mine, :] = (normed * row_of(r.second_gain) + row_of(r.second_shift)).astype(BF16)
    send_sec = t.send(r.sec2.at[mine], r.sec2.at[mine], to_near)

    hid_sends, pre_sends = [None] * 4, [None] * 4

    def hid_rows(slot):
        return pl.ds(pl.multiple_of(slot * pair + core * pad, 16), pad)

    places = {"x": (x_bit, to_x), "y": (side, to_far), "l": (z_low, to_zl), "h": (z_high, to_zh), "c": (core, to_near)}
    downs, ups = [None] * 4, [None] * 5

    def start_up(chunk):
        if fast:
            ups[chunk] = Ladder(
                t, places, r.g_up.at[chunk],
                [(name, getattr(r, "up%d%s" % (chunk, name))) for name in UP_ORDER[chunk]],
            )
            ups[chunk].start()

    qkvs, smalls, joints, finals = [None] * 3, [], [None] * 2, []
    ended, late = [], {}

    def close_down(chunk):
        r.down_low[chunk // 2, chunk % 2] = downs[chunk].take(BF16)

    def progress(point):
        if not fast:
            return
        for step in SCHEDULE.get(point, ()):
            kind, index = step[0], int(step[1:] or 0)
            if kind == "u":
                ups[index].advance()
            elif kind == "d":
                downs[index].advance()
            elif kind == "q":
                qkvs[index].advance()
            elif kind == "s":
                smalls[0].advance()
            elif kind == "c":
                close_down(index)
            elif kind == "J":
                joints[index] = Ladder(t, places, r.down_low.at[index], [("l", r.down_l.at[index])])
                joints[index].start()
            elif kind == "j":
                joints[index].advance()
            elif kind == "F":
                finals.append(Ladder(t, places, r.down_l, [("h", r.down_h)]))
                finals[0].start()
            elif kind == "b":
                downs[index].start()
            elif kind == "U":
                total = ups[index].take(F32)
                r.up_fin[0, index] = total[0:24]
                r.up_fin[1, index] = total[24:48]
                ended.append(step)
                if sum(name[0] == "U" for name in ended) == 5:
                    late["up"] = t.send(r.up_fin.at[1 - core], r.up_c, to_near)
            elif kind == "Q":
                cut = PACKED[index][1]
                r.qkv_fin[:, :, cut] = qkvs[index].take(F32).reshape(4, 24, cut.stop - cut.start)
                ended.append(step)
                if sum(name[0] == "Q" for name in ended) == 3:
                    late["qkv"] = [
                        t.send(r.qkv_fin.at[other], r.qkv_c.at[freq], (clip, other)) for other in (far, cross, near)
                    ]
                    r.qkv_c[freq] = r.qkv_fin[freq]
            elif kind == "G":
                r.down_fin[...] = finals[0].take(F32).reshape(2, 96, half)
                late["down"] = t.send(r.down_fin.at[1 - core], r.down_c, to_near)
            elif kind == "f":
                first_norm_back()

    def weight_part(chunk):
        slot = chunk % 3
        g_down = tn_dot(r.hid2[pl.ds(slot * pair, pair), :], r.grad2[...]).astype(BF16)
        spread_rows(r.g_down.at[chunk // 2, chunk % 2], g_down, "xy", DOWN_ORDER[chunk] if fast else "xy")
        if fast:
            downs[chunk] = Ladder(
                t, places, r.g_down.at[chunk // 2, chunk % 2],
                [(name, getattr(r, "down%d%s" % (chunk, name))) for name in DOWN_ORDER[chunk]],
            )
            if chunk not in HELD:
                downs[chunk].start()
        g_up = tn_dot(r.sec2[...], r.pre2[slot]).astype(BF16)
        spread_rows(r.g_up.at[chunk], g_up, "hlxy", UP_ORDER[chunk] if fast else "hlxy")
        start_up(chunk)

    for chunk in range(4):
        slot = chunk % 3
        cut = slice(768 * chunk, 768 * chunk + 768)
        up_loads[chunk].wait()
        down_loads[4 + chunk].wait()
        up, down = r.up_buf[chunk % 2], r.down_buf[chunk % 2]
        inner = dot(r.sec2[mine, :], up) + r.up_bias[cut].reshape(1, 768)
        share = 0.5 * (1.0 + lax.erf(inner * 0.7071067811865476))
        hidden = (inner * share).astype(BF16)
        slope = share + inner * (0.3989422804014327 * jnp.exp(-0.5 * inner * inner))
        d_pre = (r.d_hidden[chunk].astype(F32) * slope).astype(BF16)
        r.hid2[hid_rows(slot), :] = hidden
        r.pre_out[chunk % 2] = d_pre
        r.pre2[slot, mine, :] = r.pre_out[chunk % 2, :, my_half]
        if chunk == 0:
            send_grad.wait()
            send_sec.wait()
        else:
            hid_sends[chunk - 1].wait()
            pre_sends[chunk - 1].wait()
        hid_sends[chunk] = t.send(r.hid2.at[hid_rows(slot)], r.hid2.at[hid_rows(slot)], to_near)
        pre_sends[chunk] = t.send(r.pre_out.at[chunk % 2, :, near_half], r.pre2.at[slot, mine], to_near)
        if chunk:
            weight_part(chunk - 1)
            progress("c%d" % chunk)
        r.vec[8 + chunk : 9 + chunk, :] = column_total(d_pre.astype(F32))
        more = dot(hidden, down)
        back = nt_dot(d_pre, up)
        if chunk == 0:
            r.ff[...] = more
            r.dsec[...] = back
        else:
            r.ff[...] += more
            r.dsec[...] += back
        if chunk + 2 < 4:
            up_loads.append(load_up(chunk + 2))
            down_loads.append(load_down(chunk + 6))

    d_second = r.dsec[...]
    normed, inv_two = layer_stats(r.mid[...])
    r.vec[5:6, :] = column_total(d_second * normed)
    r.vec[6:7, :] = column_total(d_second)
    scaled = d_second * row_of(r.second_gain)
    grad_rows = r.grad[...].astype(F32)
    r.vec[7:8, :] = column_total(grad_rows)
    d_mid = grad_rows + inv_two * (
        scaled
        - jnp.mean(scaled, -1, keepdims=True)
        - normed * jnp.mean(scaled * normed, -1, keepdims=True)
    )
    r.dsec[...] = d_mid
    branch = d_mid.astype(BF16)
    r.vec[4:5, :] = column_total(branch.astype(F32))
    r.branch[...] = branch
    r.dattn[...] = nt_dot(branch, r.proj[...]).astype(BF16)
    attn_sends = [
        t.send(r.dattn.at[:, pl.ds(window_start(other), WIN)], r.dout.at[freq], (clip, other))
        for other in (far, cross, near)
    ]
    r.branch2[mine, :] = r.branch[:, my_half]
    send_branch = t.send(r.branch.at[:, near_half], r.branch2.at[mine], to_near)
    r.dout[freq] = r.dattn[:, window]
    r.grad[...] = (keep * (r.mid[...] + (r.ff[...] + row_of(r.down_bias)))).astype(BF16)
    stores = [t.load(r.grad, r.block_out_hbm)]
    hid_sends[3].wait()
    pre_sends[3].wait()
    weight_part(3)
    progress("wp3")
    send_att.wait()
    send_branch.wait()
    g_proj = tn_dot(r.att2[...], r.branch2[...]).astype(BF16)
    spread_rows(r.g_up.at[4], g_proj, "hlxy", UP_ORDER[4] if fast else "hlxy")
    start_up(4)
    progress("gproj")

    def split_tiles(values):
        low, high = values[:, 0:128], values[:, 128:256]
        return jnp.where(core == 0, low, high), jnp.where(core == 0, high, low)

    def qkv_part(cut, parts):
        g_qkv = tn_dot(r.first[...], r.hid2[0:slots, cut]).astype(BF16)
        for part in parts:
            place = getattr(r, "g_qkv%d" % part)
            spread_rows(place, g_qkv[:, PACKED[part][0]], "hlx", QKV_ORDER[part] if fast else "hlx")
            if fast:
                qkvs[part] = Ladder(
                    t, places, place, [(name, getattr(r, "qkv%d%s" % (part, name))) for name in QKV_ORDER[part]]
                )
                qkvs[part].start()

    def finish(small):
        late["up"].wait()
        for chunk in range(5):
            place = r.up_grad if chunk < 4 else r.proj_grad
            base = 768 * (chunk % 4)
            place[:, pl.ds(pl.multiple_of(base + half * core, 128), half)] = r.up_fin[core, chunk]
            place[:, pl.ds(pl.multiple_of(base + half * (1 - core), 128), half)] = r.up_c[chunk]
        stores.append(t.load(r.up_grad, r.up_grad_hbm))
        stores.append(t.load(r.proj_grad, r.proj_grad_hbm))
        for copy in late["qkv"]:
            copy.wait()
        low_lanes = lax.broadcasted_iota(jnp.int32, (1, 128), 1) < 64
        for other in range(2):
            left, right = r.qkv_c[2 * other], r.qkv_c[2 * other + 1]
            mixed = jnp.where(low_lanes, left[:, 256:384], right[:, 256:384])
            turned = jnp.where(low_lanes, right[:, 256:384], left[:, 256:384])
            base = 384 * other
            r.qkv_grad[:, base : base + 128] = left[:, 0:128]
            r.qkv_grad[:, base + 128 : base + 256] = mixed
            r.qkv_grad[:, base + 256 : base + 384] = right[:, 0:128]
            base += 768
            r.qkv_grad[:, base : base + 128] = left[:, 128:256]
            r.qkv_grad[:, base + 128 : base + 256] = pltpu.roll(turned, 64, 1)
            r.qkv_grad[:, base + 256 : base + 384] = right[:, 128:256]
            base += 768
            r.qkv_grad[:, base : base + 128] = left[:, 384:512]
            r.qkv_grad[:, base + 128 : base + 256] = left[:, 512:640] + right[:, 384:512]
            r.qkv_grad[:, base + 256 : base + 384] = right[:, 512:640]
        stores.append(t.load(r.qkv_grad, r.qkv_grad_hbm))
        r.small_fin[...] = small.take(F32)
        stores.append(t.load(r.small_fin, r.small_fin_hbm))
        late["down"].wait()
        r.down_grad[:, my_half] = r.down_fin[core]
        r.down_grad[:, near_half] = r.down_c[...]
        stores.append(t.load(r.down_grad, r.down_grad_hbm))

    whole_q, part_q = split_tiles(r.wide[:, 0:WIN].astype(F32))
    whole_k, part_k = split_tiles(r.wide[:, WIN : 2 * WIN].astype(F32))
    lane = lax.broadcasted_iota(jnp.int32, (1, 128), 1)
    own_part = jnp.where(core == 0, lane, 127 - lane) < 64
    r.up_buf[0, :, 0:128] = whole_q.astype(BF16)
    r.up_buf[0, :, 128:256] = whole_k.astype(BF16)
    r.up_buf[0, :, 256:384] = jnp.where(own_part, part_q, pltpu.roll(part_k, 64, 1)).astype(BF16)

    blocks = (side, 1 - side)
    head_rows = [pl.ds(pl.multiple_of(64 * core + 64 * head, 64), 64) for head in range(3)]
    for turn in range(2):
        block = blocks[turn]
        at = pl.ds(pl.multiple_of(block * pair, 16), pair)
        if turn == 0:
            attn_sends[2].wait()
        else:
            attn_sends[0].wait()
            attn_sends[1].wait()
            progress("t1")
        grads = jnp.concatenate([r.dout[2 * block].astype(F32), r.dout[2 * block + 1].astype(F32)], axis=0)
        scales = jnp.zeros((pair, WIN), F32)
        for head in range(3):
            scales = jnp.where(head_lanes(core, head), r.inv[at, head : head + 1], scales)
        grads = grads * scales
        r.dscaled[...] = grads.astype(BF16)
        r.qt[...] = r.q[at, :].astype(F32).T.astype(BF16)
        r.dot_t[...] = grads.T.astype(BF16)
        products = grads * r.out[at, :].astype(F32)
        dq_total = jnp.zeros((pair, WIN), F32)

        def value_part(head):
            if turn == 1:
                exp_loads[head].wait()
            r.dvt[head_rows[head], :] += dot(r.dot_t[head_rows[head], :], r.exps[head])

        if turn == 1:
            for head in range(3):
                value_part(head)
            r.hid2[0:slots, 2 * WIN : 3 * WIN] = r.dvt[...].T.astype(BF16)
            qkv_part(slice(2 * WIN, 3 * WIN), (2,))
            progress("gv")
        for head in range(3):
            lanes = head_lanes(core, head)
            mean = jnp.sum(jnp.where(lanes, products, 0.0), -1, keepdims=True)
            high = mean.astype(BF16).astype(F32)
            fill = jnp.where(spare_lane(core, 0), -high, jnp.where(spare_lane(core, 1), high - mean, 0.0))
            d_head = jnp.where(lanes, r.dscaled[...].astype(F32), fill).astype(BF16)
            if turn == 0:
                value_part(head)
            d_prob = nt_dot(d_head, r.v[...])
            d_score = (r.exps[head].astype(F32) * d_prob).astype(BF16)
            dq_total = jnp.where(lanes, dot(d_score, r.k[...]), dq_total)
            r.dkt[head_rows[head], :] += dot(r.qt[head_rows[head], :], d_score)
            if turn == 0:
                exp_loads.append(t.load(r.exp_hbm.at[head], r.exps.at[head]))
        dq_low = (dq_total * 0.125).astype(BF16).astype(F32)
        r.vec[2:3, window] += column_total(dq_low)
        whole_tile, part_tile = split_tiles(dq_low)
        r.hid2[at, 0:128] = whole_tile.astype(BF16)
        r.hid2[at, 256:384] = part_tile.astype(BF16)
        if turn == 1:
            progress("t12")
    whole_tile, part_tile = split_tiles(r.dkt[...].T)
    r.hid2[0:slots, 128:256] = whole_tile.astype(BF16)
    r.hid2[0:slots, 256:384] = add_low(r.hid2[0:slots, 256:384], pltpu.roll(part_tile, 64, 1))
    r.vec[3:4, window] = column_total(r.hid2[0:slots, 2 * WIN : 3 * WIN].astype(F32))

    def first_back(slot):
        at = pl.ds(pl.multiple_of(slot * pad, 16), pad)
        d_first = nt_dot(r.hid2[at, 0:384], r.up_buf[0, :, 0:384]) + nt_dot(r.hid2[at, 2 * WIN :], r.wide[:, 2 * WIN :])
        normed_one, inv_one = layer_stats(r.tok[slot].astype(F32))
        r.vec[0:1, :] += column_total(d_first * normed_one)
        r.vec[1:2, :] += column_total(d_first)
        return d_first, normed_one, inv_one

    r.sec2[0:pad, :] = first_back(cross)[0].astype(BF16)
    send_cross = t.send(r.sec2.at[pl.ds(0, pad)], r.first_near.at[0], to_near)
    r.branch[...] = first_back(far)[0].astype(BF16)
    progress("fb")
    send_cross.wait()
    r.branch[...] = add_low(r.branch[...], r.first_near[0])
    send_far = t.send(r.branch, r.first_far, to_far)
    qkv_part(slice(0, 384), (1, 0))
    progress("gk")
    r.sec2[pad:pair, :] = first_back(near)[0].astype(BF16)
    send_first = t.send(r.sec2.at[pl.ds(pad, pad)], r.first_near.at[1], to_near)
    own_first, normed_one, inv_one = first_back(freq)
    r.ff[...] = own_first

    def first_norm_back():
        send_first.wait()
        send_far.wait()
        d_first = r.ff[...] + r.first_near[1].astype(F32) + r.first_far[...].astype(F32)
        scaled = d_first * row_of(r.first_gain)
        r.dattn[...] = (
            r.dsec[...]
            + inv_one
            * (
                scaled
                - jnp.mean(scaled, -1, keepdims=True)
                - normed_one * jnp.mean(scaled * normed_one, -1, keepdims=True)
            )
        ).astype(BF16)
        stores.append(t.load(r.dattn, r.grad_tok_hbm))

    if fast:
        biases = [lane_cut(r.vec, 8, 96 * index, 96) for index in range(8)]
        for index in range(32):
            at = tuple((index >> bit) & 1 for bit in range(5))
            r.small[at + (slice(0, 8), slice(None))] = lane_cut(r.vec, 0, 24 * index, 24)
            r.small[at + (slice(8, 16), slice(None))] = biases[index % 8]
        small = Ladder(t, places, r.small, [(name, getattr(r, "small_" + name)) for name in "cyxlh"])
        small.start()
        smalls.append(small)
        progress("tail")
    else:
        first_norm_back()
    if fast:
        finish(small)
    for store in stores:
        store.wait()


def layer_call(fast, tokens, grad_out, keep, lengths, vectors, weights):
    rows, width = tokens.shape[1:]
    pad = -(-rows // 16) * 16
    slots, pair, half = GROUP * pad, 2 * pad, width // 2
    wide = 4 * width
    sd, vm = jax.ShapeDtypeStruct, pltpu.VMEM
    in_vm, in_sm, in_hbm = pl.BlockSpec(memory_space=pltpu.VMEM), pl.BlockSpec(memory_space=pltpu.SMEM), pl.BlockSpec(memory_space=pl.ANY)
    ins = {
        "tok_ref": (tokens, in_vm), "grad_ref": (grad_out, in_vm), "keep_ref": (keep, in_sm), "length_ref": (lengths, in_sm),
    }
    for name, value in vectors.items():
        ins[name + "_hbm"] = (value, in_hbm)
    for name, value in weights.items():
        ins[name] = (value, in_hbm)
    outs = {"block_out_hbm": sd((pad, width), BF16), "grad_tok_hbm": sd((pad, width), BF16), "exp_hbm": sd((3, pair, slots), BF16)}
    if fast:
        outs.update(
            qkv_grad_hbm=sd((24, 3 * width), F32), proj_grad_hbm=sd((24, width), F32), up_grad_hbm=sd((24, wide), F32),
            down_grad_hbm=sd((96, width), F32), small_fin_hbm=sd((16, 128), F32),
        )
    else:
        outs.update(
            g_qkv0=sd((2, 2, 2, 96, 128), BF16), g_qkv1=sd((2, 2, 2, 96, WIN), BF16), g_qkv2=sd((2, 2, 2, 96, WIN), BF16), g_up=sd((5, 2, 2, 2, 2, 48, half), BF16),
            g_down=sd((2, 2, 2, 2, 192, half), BF16), vec=sd((16, width), F32),
        )
    scratch = {
        "proj": vm((width, width), BF16), "up_buf": vm((2, width, width), BF16), "down_buf": vm((2, width, width), BF16),
        "q": vm((slots, WIN), BF16), "k": vm((slots, WIN), BF16), "v": vm((slots, WIN), BF16),
        "inv": vm((slots, 128), F32), "out": vm((slots, WIN), BF16), "attn_in": vm((GROUP, pad, WIN), BF16), "wide": vm((width, 3 * WIN), BF16), "first": vm((slots, width), BF16),
        "tok": vm((GROUP, pad, width), BF16),
        "mid": vm((pad, width), F32), "grad": vm((pad, width), BF16), "d_hidden": vm((4, pad, width), BF16),
        "ff": vm((pad, width), F32), "dsec": vm((pad, width), F32),
        "grad2": vm((pair, half), BF16), "att2": vm((pair, width), BF16), "sec2": vm((pair, width), BF16),
        "hid2": vm((3 * pair, width), BF16), "pre2": vm((3, pair, half), BF16), "pre_out": vm((2, pad, width), BF16),
        "branch": vm((pad, width), BF16), "branch2": vm((pair, half), BF16), "dattn": vm((pad, width), BF16),
        "dout": vm((GROUP, pad, WIN), BF16), "dscaled": vm((pair, WIN), BF16), "qt": vm((WIN, pair), BF16),
        "dot_t": vm((WIN, pair), BF16), "exps": vm((3, pair, slots), BF16), "dkt": vm((WIN, slots), F32),
        "dvt": vm((WIN, slots), F32),
        "first_near": vm((2, pad, width), BF16), "first_far": vm((pad, width), BF16),
    }
    for name, value in vectors.items():
        scratch[name] = vm(value.shape, F32)
    for name, value in outs.items():
        if name not in ("block_out_hbm", "grad_tok_hbm", "exp_hbm") and name.endswith("_hbm"):
            scratch[name[:-4]] = vm(value.shape, value.dtype)
    if fast:
        scratch.update(
            vec=vm((16, width), F32),
            g_down=vm((2, 2, 2, 2, 192, half), BF16), down_low=vm((2, 2, 192, half), BF16),
            down_l=vm((2, 192, half), BF16), down_h=vm((192, half), BF16), down_fin=vm((2, 96, half), F32), down_c=vm((96, half), F32),
            g_up=vm((5, 2, 2, 2, 2, 48, half), BF16), up_fin=vm((2, 5, 24, half), F32), up_c=vm((5, 24, half), F32),
            qkv_fin=vm((4, 24, 640), F32), qkv_c=vm((4, 24, 640), F32),
            small=vm((2, 2, 2, 2, 2, 16, 128), F32), small_h=vm((16, 128), F32),
        )
        for chunk, order in enumerate(DOWN_ORDER):
            for step, name in enumerate(order):
                scratch["down%d%s" % (chunk, name)] = vm((2,) * (1 - step) + (192, half), BF16)
        for step, name in enumerate("cyxl"):
            scratch["small_" + name] = vm((2,) * (4 - step) + (16, 128), F32)
        for chunk, order in enumerate(UP_ORDER):
            for step, name in enumerate(order):
                scratch["up%d%s" % (chunk, name)] = vm((2,) * (3 - step) + (48, half), BF16)
        for part, order in enumerate(QKV_ORDER):
            size = 128 if part == 0 else WIN
            scratch["g_qkv%d" % part] = vm((2, 2, 2, 96, size), BF16)
            for step, name in enumerate(order):
                scratch["qkv%d%s" % (part, name)] = vm((2,) * (2 - step) + (96, size), BF16)
    scratch.update(
        local_sem=pltpu.SemaphoreType.DMA((56,)), send_sem=pltpu.SemaphoreType.DMA((96,)), recv_sem=pltpu.SemaphoreType.DMA((96,)),
    )
    names = [*ins, *outs, *scratch]
    results = pl.pallas_call(
        functools.partial(layer_kernel, names, rows, pad, fast),
        out_shape=tuple(outs.values()),
        in_specs=[spec for _, spec in ins.values()],
        out_specs=[in_hbm if name.endswith("_hbm") else in_vm for name in outs],
        scratch_shapes=list(scratch.values()),
        compiler_params=pltpu.CompilerParams(collective_id=0, has_side_effects=True, vmem_limit_bytes=63 << 20),
        name="layer",
    )(*(value for value, _ in ins.values()))
    return {name.removesuffix("_hbm"): result for name, result in zip(outs, results)}


def close_kernel(rows, *refs):
    count = 6
    for index, (source, target) in enumerate(zip(refs[:count], refs[count + 1 :])):
        if index < 2:
            target[0] = source[0:rows, :]
        else:
            target[...] = source[...]
    small, vectors = refs[count], refs[2 * count + 1 :]
    for row, vector in enumerate(vectors[:8]):
        vector[...] = small[row, 0 : vector.shape[0]]
    quarter = lax.axis_index("clip") // 2
    biases = small[8, :]
    for index in range(1, 4):
        biases = jnp.where(quarter == index, small[8 + index, :], biases)
    vectors[8][...] = biases[0 : vectors[8].shape[0]]


def close(rows, arrays, small):
    shapes = [(1, rows, array.shape[1]) if index < 2 else array.shape for index, array in enumerate(arrays)]
    piece = arrays[0].shape[1] // 32
    outs = [jax.ShapeDtypeStruct(shape, array.dtype) for shape, array in zip(shapes, arrays)]
    outs += [jax.ShapeDtypeStruct((size,), F32) for size in [piece] * 8 + [4 * piece]]
    spec = pl.BlockSpec(memory_space=pltpu.VMEM)
    return pl.pallas_call(
        functools.partial(close_kernel, rows),
        out_shape=tuple(outs),
        in_specs=[spec] * (len(arrays) + 1),
        out_specs=[spec] * len(outs),
        name="close",
    )(*arrays, small)


def on_device(
    tokens, grad_out, freq_keep, lengths, first_gain, first_shift, qkv_weight, query_bias, value_bias, proj_weight,
    proj_bias, second_gain, second_shift, up_weight, up_bias, down_weight, down_bias,
):
    rows, width = tokens.shape[1:]
    clips = lax.axis_size("clip")
    freq = lax.axis_index("freq")
    fast = clips == 8
    got = layer_call(
        fast, tokens, grad_out, freq_keep, lengths,
        dict(
            first_gain=first_gain, first_shift=first_shift, query_bias=query_bias, value_bias=value_bias, proj_bias=proj_bias, second_gain=second_gain, second_shift=second_shift,
            up_bias=up_bias, down_bias=down_bias,
        ),
        dict(proj_hbm=proj_weight, up_hbm=up_weight, down_hbm=down_weight, qkv_hbm=qkv_weight),
    )
    if fast:
        names = ("block_out", "grad_tok", "qkv_grad", "proj_grad", "up_grad", "down_grad")
        results = close(rows, [got[name] for name in names], got["small_fin"])
        block_out, grad_tok, mats, vectors, up_bias_grad = results[0], results[1], results[2:6], results[6:14], results[14]
    else:
        half, core = width // 2, freq % 2
        block_out, grad_tok = got["block_out"][None, :rows], got["grad_tok"][None, :rows]

        def scatter(whole):
            return lax.psum_scatter(whole, ("clip", "freq"), scatter_dimension=0, tiled=True)

        def spread(part):
            placed = jnp.zeros((part.shape[0], 2, half), F32)
            placed = lax.dynamic_update_slice(placed, part.astype(F32)[:, None], (0, core, 0))
            return placed.reshape(part.shape[0], width)

        ups = got["g_up"].reshape(5, width, half)
        up = jnp.concatenate([spread(ups[chunk]) for chunk in range(4)], axis=1)
        start = (freq // 2) * 384 + (freq % 2) * 128
        part_qk, g_qk, g_v = (got["g_qkv%d" % part].reshape(width, -1).astype(F32) for part in range(3))
        own_part = (jnp.arange(128) < 64) == (core == 0)
        parts = jnp.where(own_part, part_qk, 0.0), jnp.where(own_part, jnp.roll(part_qk, 64, 1), 0.0)
        windows = [
            jnp.where(core == 0, jnp.concatenate([whole, part], 1), jnp.concatenate([part, whole], 1))
            for whole, part in zip((g_qk[:, :128], g_qk[:, 128:]), parts)
        ]
        qkv = jnp.concatenate(
            [lax.dynamic_update_slice(jnp.zeros((width, width), F32), part, (0, start)) for part in (*windows, g_v)], axis=1
        )
        mats = scatter(qkv), scatter(spread(ups[4])), scatter(up), scatter(spread(got["g_down"].reshape(4 * width, half)))
        vectors = [scatter(got["vec"][row]) for row in range(8)]
        up_bias_grad = scatter(got["vec"][8:12].reshape(-1))
    qkv_grad, proj_grad, up_grad, down_grad = mats
    gain_one, shift_one, query, value, proj, gain_two, shift_two, down = vectors
    return (
        block_out, grad_tok, gain_one, shift_one, qkv_grad, query, value, proj_grad, proj,
        gain_two, shift_two, up_grad, up_bias_grad, down_grad, down,
    )


def solution(mesh):
    acts, both = P("clip", "freq", None), ("clip", "freq")
    mat, vec = P(both, None), P(both)
    return jax.shard_map(
        on_device,
        mesh=mesh,
        in_specs=(acts, acts, P("clip", None), P("clip")) + (P(),) * 13,
        out_specs=(acts, acts, vec, vec, mat, vec, vec, mat, vec, vec, vec, mat, vec, mat, vec),
        check_vma=False,
    )
```

```python
import functools
import types

import jax
import jax.numpy as jnp
from jax import lax
from jax.experimental import pallas as pl
from jax.experimental.pallas import tpu as pltpu
from jax.sharding import PartitionSpec as P

HEADS = 12
HEAD_DIM = 64
TIME_COLS = 99
EPS = 1e-06
F32 = jnp.float32
BF16 = jnp.bfloat16
MESH = pl.DeviceIdType.MESH
NT = (((1,), (1,)), ((), ()))
TN = (((0,), (0,)), ((), ()))
WIN = 256
GROUP = 4


def nt_dot(left, right):
    return lax.dot_general(left, right, NT, preferred_element_type=F32)


def tn_dot(left, right):
    return lax.dot_general(left, right, TN, preferred_element_type=F32)


def dot(left, right):
    return jnp.dot(left, right, preferred_element_type=F32)


def row_of(vector_ref):
    return vector_ref[...].reshape(1, -1)


def flip(index, stride):
    return index + stride - 2 * stride * ((index // stride) % 2)


def window_start(freq):
    return pl.multiple_of((freq // 2) * 384 + (freq % 2) * 128, 128)


def layer_stats(values):
    center = values - jnp.mean(values, -1, keepdims=True)
    inv_std = lax.rsqrt(jnp.mean(center * center, -1, keepdims=True) + EPS)
    return center * inv_std, inv_std


def head_lanes(core, head):
    lane = lax.broadcasted_iota(jnp.int32, (1, WIN), 1)
    first = 64 * core + 64 * head
    return (lane >= first) & (lane < first + 64)


def spare_lane(core, which):
    lane = lax.broadcasted_iota(jnp.int32, (1, WIN), 1)
    return lane == 192 * (1 - core) + which


def live_rows(shape, freq, keep_ref, length_ref, rows, first=0):
    slot = lax.broadcasted_iota(jnp.int32, shape, 0) + first
    live = jnp.zeros(shape, F32)
    per = rows // TIME_COLS
    for row in range(per):
        column = slot - row * TIME_COLS
        inside = (column >= 0) & (column < TIME_COLS) & (column < length_ref[0])
        kept = (keep_ref[0, freq * per + row] > 0).astype(F32)
        live = jnp.where(inside, kept, live)
    return live


DOWN_ORDER = ("xy", "yx", "xy", "yx")
UP_ORDER = ("lhyx", "xlyh", "lyxh", "xylh", "lxyh")
QKV_ORDER = ("xlh", "lxh", "lhx")
VECTORS = (
    "first_gain", "first_shift", "query_bias", "value_bias", "proj_bias", "second_gain", "second_shift", "up_bias", "down_bias",
)
PACKED = ((slice(256, 384), slice(256, 384)), (slice(0, 256), slice(0, 256)), (slice(0, 256), slice(384, 640)))
HELD = (3,)
SCHEDULE = {
    "wp3": ("u0",),
    "t00": ("d0", "d1",),
    "t1": ("b3", "u2",),
    "gv": ("u0",),
    "t10": ("c0",),
    "t11": ("u1",),
    "t12": ("u4",),
    "fb": ("c1", "J0", "d2",),
    "gk": ("u0", "u2", "q2",),
    "nb": ("u1", "u3", "u4",),
    "ob": ("d3",),
    "tail": ("U0", "j0", "s", "u2", "q0", "q2", "c3", "U2", "q1", "c2", "J1", "Q2", "q0", "u1", "u4", "s", "q1", "u3", "Q0", "s", "U1", "U4", "j1", "F", "s", "Q1", "f", "u3", "U3", "G",),
}


class Transfers:
    def __init__(self, local_sem, send_sem, recv_sem):
        self.local_sem, self.send_sem, self.recv_sem = local_sem, send_sem, recv_sem
        self.locals, self.remotes = 0, 0

    def load(self, source, target):
        copy = pltpu.make_async_copy(source, target, self.local_sem.at[self.locals])
        self.locals += 1
        copy.start()
        return copy

    def send(self, source, target, device):
        copy = pltpu.make_async_remote_copy(
            src_ref=source, dst_ref=target, send_sem=self.send_sem.at[self.remotes],
            recv_sem=self.recv_sem.at[self.remotes], device_id=device, device_id_type=MESH,
        )
        self.remotes += 1
        copy.start()
        return copy


def lane_cut(ref, row, first, count):
    base, turn = first // 128 * 128, first % 128
    if turn + count <= 128:
        return pltpu.roll(ref[row : row + 8, base : base + 128], (128 - turn) % 128, 1)
    return pltpu.roll(ref[row : row + 8, base : base + 256], 256 - turn, 1)[:, 0:128]


def column_total(values):
    return jnp.sum(values, axis=0, keepdims=True)


def add_low(left, right):
    return (left.astype(F32) + right.astype(F32)).astype(BF16)


class Ladder:
    def __init__(self, transfers, places, whole, buffers):
        self.transfers, self.places, self.whole = transfers, places, whole
        self.buffers, self.step = buffers, 0

    def start(self):
        name, buffer = self.buffers[self.step]
        bit, partner = self.places[name]
        self.copy = self.transfers.send(self.whole.at[1 - bit], buffer, partner)

    def take(self, dtype):
        name, buffer = self.buffers[self.step]
        self.copy.wait()
        return (buffer[...].astype(F32) + self.whole[self.places[name][0]].astype(F32)).astype(dtype)

    def advance(self):
        buffer = self.buffers[self.step][1]
        buffer[...] = self.take(buffer.dtype)
        self.whole, self.step = buffer, self.step + 1
        if self.step < len(self.buffers):
            self.start()


def spread_rows(target, rows, axes, order):
    size = rows.shape[0] >> len(axes)
    for index in range(1 << len(axes)):
        bits = {name: (index >> (len(axes) - 1 - at)) & 1 for at, name in enumerate(axes)}
        target[tuple(bits[name] for name in order)] = rows[index * size : index * size + size]


def layer_kernel(names, rows, pad, fast, *refs):
    r = types.SimpleNamespace(**dict(zip(names, refs)))
    clip, freq = lax.axis_index("clip"), lax.axis_index("freq")
    core, side = freq % 2, freq // 2
    near, far, cross = flip(freq, 1), flip(freq, 2), flip(flip(freq, 1), 2)
    x_bit, z_low, z_high = clip % 2, (clip // 2) % 2, clip // 4
    to_near, to_far, to_cross = (clip, near), (clip, far), (clip, cross)
    to_x, to_zl, to_zh = (flip(clip, 1), freq), (flip(clip, 2), freq), (flip(clip, 4), freq)
    slots = GROUP * pad
    pair = 2 * pad
    half = 384
    t = Transfers(r.local_sem, r.send_sem, r.recv_sem)
    mine = pl.ds(pl.multiple_of(core * pad, 16), pad)
    my_half = pl.ds(pl.multiple_of(core * half, 128), half)
    near_half = pl.ds(pl.multiple_of((1 - core) * half, 128), half)
    start = window_start(freq)
    window = pl.ds(start, WIN)

    def load_down(chunk):
        return t.load(r.down_hbm.at[pl.ds(768 * (chunk % 4), 768), :], r.down_buf.at[chunk % 2])

    def load_up(chunk):
        return t.load(r.up_hbm.at[:, pl.ds(768 * chunk, 768)], r.up_buf.at[chunk % 2])

    vector_loads = [t.load(getattr(r, name + "_hbm"), getattr(r, name)) for name in VECTORS]
    load_wide = [
        t.load(r.qkv_hbm.at[:, pl.ds(pl.multiple_of(start + 768 * part, 128), WIN)], r.wide.at[:, pl.ds(WIN * part, WIN)])
        for part in range(3)
    ]
    partners = [to_near, to_far, to_cross] + ([to_x, to_zl, to_zh] if fast else [])
    barrier = pltpu.get_barrier_semaphore()
    for device in partners:
        pl.semaphore_signal(barrier, inc=1, device_id=device, device_id_type=MESH)
    r.tok[freq, pad - 16 : pad, :] = jnp.zeros((16, 768), BF16)
    r.tok[freq, 0:rows, :] = r.tok_ref[0]
    pl.semaphore_wait(barrier, len(partners))

    cuts = [(0, 80), (80, 80), (160, 80), (240, pad - 240)]
    far_copies = [
        t.send(r.tok.at[freq, pl.ds(first, count)], r.tok.at[freq, pl.ds(first, count)], to_far) for first, count in cuts
    ]
    near_copy = t.send(r.tok.at[freq], r.tok.at[freq], to_near)
    load_proj = t.load(r.proj_hbm, r.proj)
    down_loads = [load_down(0), load_down(1)]
    up_loads = [load_up(0), load_up(1)]

    def project(slot, first=0, count=pad):
        span = pl.ds(pl.multiple_of(slot * pad + first, 16), count)
        normed_one, _ = layer_stats(r.tok[slot, first : first + count].astype(F32))
        low = (normed_one * row_of(r.first_gain) + row_of(r.first_shift)).astype(BF16)
        r.first[span, :] = low
        live = live_rows((count, 1), slot, r.keep_ref, r.length_ref, rows, first)
        queries = (dot(low, r.wide[:, 0:WIN]) + r.query_bias[window].reshape(1, WIN)).astype(BF16).astype(F32) * 0.125
        keys = dot(low, r.wide[:, WIN : 2 * WIN])
        values = dot(low, r.wide[:, 2 * WIN : 3 * WIN]) + r.value_bias[window].reshape(1, WIN)
        one = spare_lane(core, 0)
        both = one | spare_lane(core, 1)
        r.q[span, :] = jnp.where(one, 1.0, queries).astype(BF16)
        r.k[span, :] = jnp.where(one, (live - 1.0) * 1e30, keys).astype(BF16)
        r.v[span, :] = jnp.where(both, 1.0, values).astype(BF16)

    for load in vector_loads + load_wide:
        load.wait()
    project(freq)
    near_copy.wait()
    project(near)
    keep = live_rows((pad, 1), freq, r.keep_ref, r.length_ref, rows)
    r.mid[pad - 16 : pad, :] = jnp.zeros((16, 768), F32)
    r.mid[0:rows, :] = r.tok_ref[0].astype(F32)
    r.grad[pad - 16 : pad, :] = jnp.zeros((16, 768), BF16)
    r.grad[0:rows, :] = r.grad_ref[0]
    r.grad[...] = (r.grad[...].astype(F32) * keep).astype(BF16)
    r.vec[...] = jnp.zeros_like(r.vec)
    r.dkt[...] = jnp.zeros_like(r.dkt)
    r.dvt[...] = jnp.zeros_like(r.dvt)
    r.grad2[mine, :] = r.grad[:, my_half]
    send_grad = t.send(r.grad.at[:, near_half], r.grad2.at[mine], to_near)
    for chunk in range(4):
        down_loads[chunk].wait()
        r.d_hidden[chunk] = nt_dot(r.grad[...], r.down_buf[chunk % 2]).astype(BF16)
        down_loads.append(load_down(chunk + 2))
    forwards = []

    def hand_on(part):
        first, count = cuts[part]
        far_copies[part].wait()
        forwards.append(t.send(r.tok.at[far, pl.ds(first, count)], r.tok.at[far, pl.ds(first, count)], to_near))

    hand_on(0)
    hand_on(1)
    project(far, 0, 160)
    forwards[0].wait()
    forwards[1].wait()
    hand_on(2)
    project(cross, 0, 160)
    hand_on(3)
    project(far, 160, pad - 160)
    forwards[2].wait()
    forwards[3].wait()
    project(cross, 160, pad - 160)

    out_sends, exp_saves, exp_loads = [], [], []

    def scores_of(unit):
        slot, head = (far, cross, near, freq)[unit // 3], unit % 3
        q_rows = r.q[pl.ds(pl.multiple_of(slot * pad, 16), pad), :]
        q_head = jnp.where(head_lanes(core, head) | spare_lane(core, 0), q_rows, jnp.zeros_like(q_rows))
        return nt_dot(q_head, r.k[...])

    ahead = scores_of(0)
    for turn, slot in enumerate((far, cross, near, freq)):
        span = pl.ds(pl.multiple_of(slot * pad, 16), pad)
        stage = pl.ds(pl.multiple_of((slot % 2) * pad, 16), pad)
        total = jnp.zeros((pad, WIN), F32)
        inverse = jnp.zeros((pad, 128), F32)
        if turn >= 2:
            for save in exp_saves[3 * (3 - turn) : 3 * (3 - turn) + 3]:
                save.wait()
        for head in range(3):
            lanes = head_lanes(core, head)
            scores = ahead
            if 3 * turn + head < 11:
                ahead = scores_of(3 * turn + head + 1)
            exps = jnp.exp(scores - jnp.max(scores, -1, keepdims=True)).astype(BF16)
            r.exps[head, stage, :] = exps
            mixed = dot(exps, r.v[...])
            scale = 1.0 / jnp.sum(jnp.where(spare_lane(core, 0), mixed, 0.0), -1, keepdims=True)
            total = jnp.where(lanes, mixed * scale, total)
            inverse = jnp.where(lax.broadcasted_iota(jnp.int32, (1, 128), 1) == head, scale, inverse)
            if head:
                tile = slice(128 * head - 128, 128 * head)
                if turn == 3:
                    r.attn_in[freq, :, tile] = total[:, tile].astype(BF16)
                else:
                    lanes_out = pl.ds(128 * head - 128, 128)
                    r.out[span, tile] = total[:, tile].astype(BF16)
                    out_sends.append(
                        t.send(r.out.at[span, lanes_out], r.attn_in.at[freq, :, lanes_out], (clip, slot))
                    )
        if turn < 2:
            for head in range(3):
                exp_saves.append(t.load(r.exps.at[head, stage], r.exp_hbm.at[head, stage]))
        r.inv[span, :] = inverse
        if turn == 3:
            r.out[span, :] = total.astype(BF16)
    for copy in out_sends:
        copy.wait()
    for side_in in range(2):
        left, right = r.attn_in[2 * side_in], r.attn_in[2 * side_in + 1]
        base = 384 * side_in
        r.att2[mine, base : base + 128] = left[:, 0:128]
        r.att2[mine, base + 128 : base + 256] = add_low(left[:, 128:256], right[:, 0:128])
        r.att2[mine, base + 256 : base + 384] = right[:, 128:256]
    send_att = t.send(r.att2.at[mine], r.att2.at[mine], to_near)

    load_proj.wait()
    middle = r.mid[...] + (dot(r.att2[mine, :], r.proj[...]) + row_of(r.proj_bias))
    r.mid[...] = middle
    normed, inv_two = layer_stats(middle)
    r.sec2[mine, :] = (normed * row_of(r.second_gain) + row_of(r.second_shift)).astype(BF16)
    send_sec = t.send(r.sec2.at[mine], r.sec2.at[mine], to_near)

    hid_sends, pre_sends = [None] * 4, [None] * 4

    def hid_rows(slot):
        return pl.ds(pl.multiple_of(slot * pair + core * pad, 16), pad)

    places = {"x": (x_bit, to_x), "y": (side, to_far), "l": (z_low, to_zl), "h": (z_high, to_zh), "c": (core, to_near)}
    downs, ups = [None] * 4, [None] * 5

    def start_up(chunk):
        if fast:
            ups[chunk] = Ladder(
                t, places, r.g_up.at[chunk],
                [(name, getattr(r, "up%d%s" % (chunk, name))) for name in UP_ORDER[chunk]],
            )
            ups[chunk].start()

    qkvs, smalls, joints, finals = [None] * 3, [], [None] * 2, []
    ended, late = [], {}

    def close_down(chunk):
        r.down_low[chunk // 2, chunk % 2] = downs[chunk].take(BF16)

    def progress(point):
        if not fast:
            return
        for step in SCHEDULE.get(point, ()):
            kind, index = step[0], int(step[1:] or 0)
            if kind == "u":
                ups[index].advance()
            elif kind == "d":
                downs[index].advance()
            elif kind == "q":
                qkvs[index].advance()
            elif kind == "s":
                smalls[0].advance()
            elif kind == "c":
                close_down(index)
            elif kind == "J":
                joints[index] = Ladder(t, places, r.down_low.at[index], [("l", r.down_l.at[index])])
                joints[index].start()
            elif kind == "j":
                joints[index].advance()
            elif kind == "F":
                finals.append(Ladder(t, places, r.down_l, [("h", r.down_h)]))
                finals[0].start()
            elif kind == "b":
                downs[index].start()
            elif kind == "U":
                total = ups[index].take(F32)
                r.up_fin[0, index] = total[0:24]
                r.up_fin[1, index] = total[24:48]
                ended.append(step)
                if sum(name[0] == "U" for name in ended) == 5:
                    late["up"] = t.send(r.up_fin.at[1 - core], r.up_c, to_near)
            elif kind == "Q":
                cut = PACKED[index][1]
                r.qkv_fin[:, :, cut] = qkvs[index].take(F32).reshape(4, 24, cut.stop - cut.start)
                ended.append(step)
                if sum(name[0] == "Q" for name in ended) == 3:
                    late["qkv"] = [
                        t.send(r.qkv_fin.at[other], r.qkv_c.at[freq], (clip, other)) for other in (far, cross, near)
                    ]
                    r.qkv_c[freq] = r.qkv_fin[freq]
            elif kind == "G":
                r.down_fin[...] = finals[0].take(F32).reshape(2, 96, half)
                late["down"] = t.send(r.down_fin.at[1 - core], r.down_c, to_near)
            elif kind == "f":
                first_norm_back()

    def weight_part(chunk):
        slot = chunk % 3
        g_down = tn_dot(r.hid2[pl.ds(slot * pair, pair), :], r.grad2[...]).astype(BF16)
        spread_rows(r.g_down.at[chunk // 2, chunk % 2], g_down, "xy", DOWN_ORDER[chunk] if fast else "xy")
        if fast:
            downs[chunk] = Ladder(
                t, places, r.g_down.at[chunk // 2, chunk % 2],
                [(name, getattr(r, "down%d%s" % (chunk, name))) for name in DOWN_ORDER[chunk]],
            )
            if chunk not in HELD:
                downs[chunk].start()
        g_up = tn_dot(r.sec2[...], r.pre2[slot]).astype(BF16)
        spread_rows(r.g_up.at[chunk], g_up, "hlxy", UP_ORDER[chunk] if fast else "hlxy")
        start_up(chunk)

    for chunk in range(4):
        slot = chunk % 3
        cut = slice(768 * chunk, 768 * chunk + 768)
        up_loads[chunk].wait()
        down_loads[4 + chunk].wait()
        up, down = r.up_buf[chunk % 2], r.down_buf[chunk % 2]
        inner = dot(r.sec2[mine, :], up) + r.up_bias[cut].reshape(1, 768)
        share = 0.5 * (1.0 + lax.erf(inner * 0.7071067811865476))
        hidden = (inner * share).astype(BF16)
        slope = share + inner * (0.3989422804014327 * jnp.exp(-0.5 * inner * inner))
        d_pre = (r.d_hidden[chunk].astype(F32) * slope).astype(BF16)
        r.hid2[hid_rows(slot), :] = hidden
        r.pre_out[chunk % 2] = d_pre
        r.pre2[slot, mine, :] = r.pre_out[chunk % 2, :, my_half]
        if chunk == 0:
            send_grad.wait()
            send_sec.wait()
        else:
            hid_sends[chunk - 1].wait()
            pre_sends[chunk - 1].wait()
        hid_sends[chunk] = t.send(r.hid2.at[hid_rows(slot)], r.hid2.at[hid_rows(slot)], to_near)
        pre_sends[chunk] = t.send(r.pre_out.at[chunk % 2, :, near_half], r.pre2.at[slot, mine], to_near)
        if chunk:
            weight_part(chunk - 1)
            progress("c%d" % chunk)
        r.vec[8 + chunk : 9 + chunk, :] = column_total(d_pre.astype(F32))
        more = dot(hidden, down)
        back = nt_dot(d_pre, up)
        if chunk == 0:
            r.ff[...] = more
            r.dsec[...] = back
        else:
            r.ff[...] += more
            r.dsec[...] += back
        if chunk + 2 < 4:
            up_loads.append(load_up(chunk + 2))
            down_loads.append(load_down(chunk + 6))

    d_second = r.dsec[...]
    normed, inv_two = layer_stats(r.mid[...])
    r.vec[5:6, :] = column_total(d_second * normed)
    r.vec[6:7, :] = column_total(d_second)
    scaled = d_second * row_of(r.second_gain)
    grad_rows = r.grad[...].astype(F32)
    r.vec[7:8, :] = column_total(grad_rows)
    d_mid = grad_rows + inv_two * (
        scaled
        - jnp.mean(scaled, -1, keepdims=True)
        - normed * jnp.mean(scaled * normed, -1, keepdims=True)
    )
    r.dsec[...] = d_mid
    branch = d_mid.astype(BF16)
    r.vec[4:5, :] = column_total(branch.astype(F32))
    r.branch[...] = branch
    r.dattn[...] = nt_dot(branch, r.proj[...]).astype(BF16)
    attn_sends = [
        t.send(r.dattn.at[:, pl.ds(window_start(other), WIN)], r.dout.at[freq], (clip, other))
        for other in (far, cross, near)
    ]
    r.branch2[mine, :] = r.branch[:, my_half]
    send_branch = t.send(r.branch.at[:, near_half], r.branch2.at[mine], to_near)
    r.dout[freq] = r.dattn[:, window]
    r.grad[...] = (keep * (r.mid[...] + (r.ff[...] + row_of(r.down_bias)))).astype(BF16)
    stores = [t.load(r.grad, r.block_out_hbm)]
    hid_sends[3].wait()
    pre_sends[3].wait()
    weight_part(3)
    progress("wp3")
    send_att.wait()
    send_branch.wait()
    g_proj = tn_dot(r.att2[...], r.branch2[...]).astype(BF16)
    spread_rows(r.g_up.at[4], g_proj, "hlxy", UP_ORDER[4] if fast else "hlxy")
    start_up(4)
    progress("gproj")

    def split_tiles(values):
        low, high = values[:, 0:128], values[:, 128:256]
        return jnp.where(core == 0, low, high), jnp.where(core == 0, high, low)

    def qkv_part(cut, parts):
        g_qkv = tn_dot(r.first[...], r.hid2[0:slots, cut]).astype(BF16)
        for part in parts:
            place = getattr(r, "g_qkv%d" % part)
            spread_rows(place, g_qkv[:, PACKED[part][0]], "hlx", QKV_ORDER[part] if fast else "hlx")
            if fast:
                qkvs[part] = Ladder(
                    t, places, place, [(name, getattr(r, "qkv%d%s" % (part, name))) for name in QKV_ORDER[part]]
                )
                qkvs[part].start()

    def finish(small):
        late["up"].wait()
        for chunk in range(5):
            place = r.up_grad if chunk < 4 else r.proj_grad
            base = 768 * (chunk % 4)
            place[:, pl.ds(pl.multiple_of(base + half * core, 128), half)] = r.up_fin[core, chunk]
            place[:, pl.ds(pl.multiple_of(base + half * (1 - core), 128), half)] = r.up_c[chunk]
        stores.append(t.load(r.up_grad, r.up_grad_hbm))
        stores.append(t.load(r.proj_grad, r.proj_grad_hbm))
        for copy in late["qkv"]:
            copy.wait()
        low_lanes = lax.broadcasted_iota(jnp.int32, (1, 128), 1) < 64
        for other in range(2):
            left, right = r.qkv_c[2 * other], r.qkv_c[2 * other + 1]
            mixed = jnp.where(low_lanes, left[:, 256:384], right[:, 256:384])
            turned = jnp.where(low_lanes, right[:, 256:384], left[:, 256:384])
            base = 384 * other
            r.qkv_grad[:, base : base + 128] = left[:, 0:128]
            r.qkv_grad[:, base + 128 : base + 256] = mixed
            r.qkv_grad[:, base + 256 : base + 384] = right[:, 0:128]
            base += 768
            r.qkv_grad[:, base : base + 128] = left[:, 128:256]
            r.qkv_grad[:, base + 128 : base + 256] = pltpu.roll(turned, 64, 1)
            r.qkv_grad[:, base + 256 : base + 384] = right[:, 128:256]
            base += 768
            r.qkv_grad[:, base : base + 128] = left[:, 384:512]
            r.qkv_grad[:, base + 128 : base + 256] = left[:, 512:640] + right[:, 384:512]
            r.qkv_grad[:, base + 256 : base + 384] = right[:, 512:640]
        stores.append(t.load(r.qkv_grad, r.qkv_grad_hbm))
        r.small_fin[...] = small.take(F32)
        stores.append(t.load(r.small_fin, r.small_fin_hbm))
        late["down"].wait()
        r.down_grad[:, my_half] = r.down_fin[core]
        r.down_grad[:, near_half] = r.down_c[...]
        stores.append(t.load(r.down_grad, r.down_grad_hbm))

    whole_q, part_q = split_tiles(r.wide[:, 0:WIN].astype(F32))
    whole_k, part_k = split_tiles(r.wide[:, WIN : 2 * WIN].astype(F32))
    lane = lax.broadcasted_iota(jnp.int32, (1, 128), 1)
    own_part = jnp.where(core == 0, lane, 127 - lane) < 64
    r.up_buf[0, :, 0:128] = whole_q.astype(BF16)
    r.up_buf[0, :, 128:256] = whole_k.astype(BF16)
    r.up_buf[0, :, 256:384] = jnp.where(own_part, part_q, pltpu.roll(part_k, 64, 1)).astype(BF16)

    blocks = (side, 1 - side)
    head_rows = [pl.ds(pl.multiple_of(64 * core + 64 * head, 64), 64) for head in range(3)]
    for turn in range(2):
        block = blocks[turn]
        at = pl.ds(pl.multiple_of(block * pair, 16), pair)
        if turn == 0:
            attn_sends[2].wait()
        else:
            attn_sends[0].wait()
            attn_sends[1].wait()
            progress("t1")
        grads = jnp.concatenate([r.dout[2 * block].astype(F32), r.dout[2 * block + 1].astype(F32)], axis=0)
        scales = jnp.zeros((pair, WIN), F32)
        for head in range(3):
            scales = jnp.where(head_lanes(core, head), r.inv[at, head : head + 1], scales)
        grads = grads * scales
        r.dscaled[...] = grads.astype(BF16)
        r.qt[...] = r.q[at, :].astype(F32).T.astype(BF16)
        r.dot_t[...] = grads.T.astype(BF16)
        products = grads * r.out[at, :].astype(F32)
        dq_total = jnp.zeros((pair, WIN), F32)

        def value_part(head):
            if turn == 1:
                exp_loads[head].wait()
            r.dvt[head_rows[head], :] += dot(r.dot_t[head_rows[head], :], r.exps[head])

        if turn == 1:
            for head in range(3):
                value_part(head)
            r.hid2[0:slots, 2 * WIN : 3 * WIN] = r.dvt[...].T.astype(BF16)
            qkv_part(slice(2 * WIN, 3 * WIN), (2,))
            progress("gv")
        for head in range(3):
            lanes = head_lanes(core, head)
            mean = jnp.sum(jnp.where(lanes, products, 0.0), -1, keepdims=True)
            high = mean.astype(BF16).astype(F32)
            fill = jnp.where(spare_lane(core, 0), -high, jnp.where(spare_lane(core, 1), high - mean, 0.0))
            d_head = jnp.where(lanes, r.dscaled[...].astype(F32), fill).astype(BF16)
            if turn == 0:
                value_part(head)
            d_prob = nt_dot(d_head, r.v[...])
            d_score = (r.exps[head].astype(F32) * d_prob).astype(BF16)
            dq_total = jnp.where(lanes, dot(d_score, r.k[...]), dq_total)
            r.dkt[head_rows[head], :] += dot(r.qt[head_rows[head], :], d_score)
            if turn == 0:
                exp_loads.append(t.load(r.exp_hbm.at[head], r.exps.at[head]))
            progress("t%d%d" % (turn, head))
        dq_low = (dq_total * 0.125).astype(BF16).astype(F32)
        r.vec[2:3, window] += column_total(dq_low)
        whole_tile, part_tile = split_tiles(dq_low)
        r.hid2[at, 0:128] = whole_tile.astype(BF16)
        r.hid2[at, 256:384] = part_tile.astype(BF16)
    whole_tile, part_tile = split_tiles(r.dkt[...].T)
    r.hid2[0:slots, 128:256] = whole_tile.astype(BF16)
    r.hid2[0:slots, 256:384] = add_low(r.hid2[0:slots, 256:384], pltpu.roll(part_tile, 64, 1))
    r.vec[3:4, window] = column_total(r.hid2[0:slots, 2 * WIN : 3 * WIN].astype(F32))

    def first_back(slot):
        at = pl.ds(pl.multiple_of(slot * pad, 16), pad)
        d_first = nt_dot(r.hid2[at, 0:384], r.up_buf[0, :, 0:384]) + nt_dot(r.hid2[at, 2 * WIN :], r.wide[:, 2 * WIN :])
        normed_one, inv_one = layer_stats(r.tok[slot].astype(F32))
        r.vec[0:1, :] += column_total(d_first * normed_one)
        r.vec[1:2, :] += column_total(d_first)
        return d_first, normed_one, inv_one

    r.sec2[0:pad, :] = first_back(cross)[0].astype(BF16)
    send_cross = t.send(r.sec2.at[pl.ds(0, pad)], r.first_near.at[0], to_near)
    r.branch[...] = first_back(far)[0].astype(BF16)
    progress("fb")
    send_cross.wait()
    r.branch[...] = add_low(r.branch[...], r.first_near[0])
    send_far = t.send(r.branch, r.first_far, to_far)
    qkv_part(slice(0, 384), (1, 0))
    progress("gk")
    r.sec2[pad:pair, :] = first_back(near)[0].astype(BF16)
    send_first = t.send(r.sec2.at[pl.ds(pad, pad)], r.first_near.at[1], to_near)
    progress("nb")
    own_first, normed_one, inv_one = first_back(freq)
    r.ff[...] = own_first
    progress("ob")

    def first_norm_back():
        send_first.wait()
        send_far.wait()
        d_first = r.ff[...] + r.first_near[1].astype(F32) + r.first_far[...].astype(F32)
        scaled = d_first * row_of(r.first_gain)
        r.dattn[...] = (
            r.dsec[...]
            + inv_one
            * (
                scaled
                - jnp.mean(scaled, -1, keepdims=True)
                - normed_one * jnp.mean(scaled * normed_one, -1, keepdims=True)
            )
        ).astype(BF16)
        stores.append(t.load(r.dattn, r.grad_tok_hbm))

    if fast:
        biases = [lane_cut(r.vec, 8, 96 * index, 96) for index in range(8)]
        for index in range(32):
            at = tuple((index >> bit) & 1 for bit in range(5))
            r.small[at + (slice(0, 8), slice(None))] = lane_cut(r.vec, 0, 24 * index, 24)
            r.small[at + (slice(8, 16), slice(None))] = biases[index % 8]
        small = Ladder(t, places, r.small, [(name, getattr(r, "small_" + name)) for name in "cyxlh"])
        small.start()
        smalls.append(small)
        progress("tail")
    else:
        first_norm_back()
    if fast:
        finish(small)
    for store in stores:
        store.wait()


def layer_call(fast, tokens, grad_out, keep, lengths, vectors, weights):
    rows, width = tokens.shape[1:]
    pad = -(-rows // 16) * 16
    slots, pair, half = GROUP * pad, 2 * pad, width // 2
    wide = 4 * width
    sd, vm = jax.ShapeDtypeStruct, pltpu.VMEM
    in_vm, in_sm, in_hbm = pl.BlockSpec(memory_space=pltpu.VMEM), pl.BlockSpec(memory_space=pltpu.SMEM), pl.BlockSpec(memory_space=pl.ANY)
    ins = {
        "tok_ref": (tokens, in_vm), "grad_ref": (grad_out, in_vm), "keep_ref": (keep, in_sm), "length_ref": (lengths, in_sm),
    }
    for name, value in vectors.items():
        ins[name + "_hbm"] = (value, in_hbm)
    for name, value in weights.items():
        ins[name] = (value, in_hbm)
    outs = {"block_out_hbm": sd((pad, width), BF16), "grad_tok_hbm": sd((pad, width), BF16), "exp_hbm": sd((3, pair, slots), BF16)}
    if fast:
        outs.update(
            qkv_grad_hbm=sd((24, 3 * width), F32), proj_grad_hbm=sd((24, width), F32), up_grad_hbm=sd((24, wide), F32),
            down_grad_hbm=sd((96, width), F32), small_fin_hbm=sd((16, 128), F32),
        )
    else:
        outs.update(
            g_qkv0=sd((2, 2, 2, 96, 128), BF16), g_qkv1=sd((2, 2, 2, 96, WIN), BF16), g_qkv2=sd((2, 2, 2, 96, WIN), BF16), g_up=sd((5, 2, 2, 2, 2, 48, half), BF16),
            g_down=sd((2, 2, 2, 2, 192, half), BF16), vec=sd((16, width), F32),
        )
    scratch = {
        "proj": vm((width, width), BF16), "up_buf": vm((2, width, width), BF16), "down_buf": vm((2, width, width), BF16),
        "q": vm((slots, WIN), BF16), "k": vm((slots, WIN), BF16), "v": vm((slots, WIN), BF16),
        "inv": vm((slots, 128), F32), "out": vm((slots, WIN), BF16), "attn_in": vm((GROUP, pad, WIN), BF16), "wide": vm((width, 3 * WIN), BF16), "first": vm((slots, width), BF16),
        "tok": vm((GROUP, pad, width), BF16),
        "mid": vm((pad, width), F32), "grad": vm((pad, width), BF16), "d_hidden": vm((4, pad, width), BF16),
        "ff": vm((pad, width), F32), "dsec": vm((pad, width), F32),
        "grad2": vm((pair, half), BF16), "att2": vm((pair, width), BF16), "sec2": vm((pair, width), BF16),
        "hid2": vm((3 * pair, width), BF16), "pre2": vm((3, pair, half), BF16), "pre_out": vm((2, pad, width), BF16),
        "branch": vm((pad, width), BF16), "branch2": vm((pair, half), BF16), "dattn": vm((pad, width), BF16),
        "dout": vm((GROUP, pad, WIN), BF16), "dscaled": vm((pair, WIN), BF16), "qt": vm((WIN, pair), BF16),
        "dot_t": vm((WIN, pair), BF16), "exps": vm((3, pair, slots), BF16), "dkt": vm((WIN, slots), F32),
        "dvt": vm((WIN, slots), F32),
        "first_near": vm((2, pad, width), BF16), "first_far": vm((pad, width), BF16),
    }
    for name, value in vectors.items():
        scratch[name] = vm(value.shape, F32)
    for name, value in outs.items():
        if name not in ("block_out_hbm", "grad_tok_hbm", "exp_hbm") and name.endswith("_hbm"):
            scratch[name[:-4]] = vm(value.shape, value.dtype)
    if fast:
        scratch.update(
            vec=vm((16, width), F32),
            g_down=vm((2, 2, 2, 2, 192, half), BF16), down_low=vm((2, 2, 192, half), BF16),
            down_l=vm((2, 192, half), BF16), down_h=vm((192, half), BF16), down_fin=vm((2, 96, half), F32), down_c=vm((96, half), F32),
            g_up=vm((5, 2, 2, 2, 2, 48, half), BF16), up_fin=vm((2, 5, 24, half), F32), up_c=vm((5, 24, half), F32),
            qkv_fin=vm((4, 24, 640), F32), qkv_c=vm((4, 24, 640), F32),
            small=vm((2, 2, 2, 2, 2, 16, 128), F32), small_h=vm((16, 128), F32),
        )
        for chunk, order in enumerate(DOWN_ORDER):
            for step, name in enumerate(order):
                scratch["down%d%s" % (chunk, name)] = vm((2,) * (1 - step) + (192, half), BF16)
        for step, name in enumerate("cyxl"):
            scratch["small_" + name] = vm((2,) * (4 - step) + (16, 128), F32)
        for chunk, order in enumerate(UP_ORDER):
            for step, name in enumerate(order):
                scratch["up%d%s" % (chunk, name)] = vm((2,) * (3 - step) + (48, half), BF16)
        for part, order in enumerate(QKV_ORDER):
            size = 128 if part == 0 else WIN
            scratch["g_qkv%d" % part] = vm((2, 2, 2, 96, size), BF16)
            for step, name in enumerate(order):
                scratch["qkv%d%s" % (part, name)] = vm((2,) * (2 - step) + (96, size), BF16)
    scratch.update(
        local_sem=pltpu.SemaphoreType.DMA((56,)), send_sem=pltpu.SemaphoreType.DMA((96,)), recv_sem=pltpu.SemaphoreType.DMA((96,)),
    )
    names = [*ins, *outs, *scratch]
    results = pl.pallas_call(
        functools.partial(layer_kernel, names, rows, pad, fast),
        out_shape=tuple(outs.values()),
        in_specs=[spec for _, spec in ins.values()],
        out_specs=[in_hbm if name.endswith("_hbm") else in_vm for name in outs],
        scratch_shapes=list(scratch.values()),
        compiler_params=pltpu.CompilerParams(collective_id=0, has_side_effects=True, vmem_limit_bytes=63 << 20),
        name="layer",
    )(*(value for value, _ in ins.values()))
    return {name.removesuffix("_hbm"): result for name, result in zip(outs, results)}


def close_kernel(rows, *refs):
    count = 6
    for index, (source, target) in enumerate(zip(refs[:count], refs[count + 1 :])):
        if index < 2:
            target[0] = source[0:rows, :]
        else:
            target[...] = source[...]
    small, vectors = refs[count], refs[2 * count + 1 :]
    for row, vector in enumerate(vectors[:8]):
        vector[...] = small[row, 0 : vector.shape[0]]
    quarter = lax.axis_index("clip") // 2
    biases = small[8, :]
    for index in range(1, 4):
        biases = jnp.where(quarter == index, small[8 + index, :], biases)
    vectors[8][...] = biases[0 : vectors[8].shape[0]]


def close(rows, arrays, small):
    shapes = [(1, rows, array.shape[1]) if index < 2 else array.shape for index, array in enumerate(arrays)]
    piece = arrays[0].shape[1] // 32
    outs = [jax.ShapeDtypeStruct(shape, array.dtype) for shape, array in zip(shapes, arrays)]
    outs += [jax.ShapeDtypeStruct((size,), F32) for size in [piece] * 8 + [4 * piece]]
    spec = pl.BlockSpec(memory_space=pltpu.VMEM)
    return pl.pallas_call(
        functools.partial(close_kernel, rows),
        out_shape=tuple(outs),
        in_specs=[spec] * (len(arrays) + 1),
        out_specs=[spec] * len(outs),
        name="close",
    )(*arrays, small)


def on_device(
    tokens, grad_out, freq_keep, lengths, first_gain, first_shift, qkv_weight, query_bias, value_bias, proj_weight,
    proj_bias, second_gain, second_shift, up_weight, up_bias, down_weight, down_bias,
):
    rows, width = tokens.shape[1:]
    clips = lax.axis_size("clip")
    freq = lax.axis_index("freq")
    fast = clips == 8
    got = layer_call(
        fast, tokens, grad_out, freq_keep, lengths,
        dict(
            first_gain=first_gain, first_shift=first_shift, query_bias=query_bias, value_bias=value_bias, proj_bias=proj_bias, second_gain=second_gain, second_shift=second_shift,
            up_bias=up_bias, down_bias=down_bias,
        ),
        dict(proj_hbm=proj_weight, up_hbm=up_weight, down_hbm=down_weight, qkv_hbm=qkv_weight),
    )
    if fast:
        names = ("block_out", "grad_tok", "qkv_grad", "proj_grad", "up_grad", "down_grad")
        results = close(rows, [got[name] for name in names], got["small_fin"])
        block_out, grad_tok, mats, vectors, up_bias_grad = results[0], results[1], results[2:6], results[6:14], results[14]
    else:
        half, core = width // 2, freq % 2
        block_out, grad_tok = got["block_out"][None, :rows], got["grad_tok"][None, :rows]

        def scatter(whole):
            return lax.psum_scatter(whole, ("clip", "freq"), scatter_dimension=0, tiled=True)

        def spread(part):
            placed = jnp.zeros((part.shape[0], 2, half), F32)
            placed = lax.dynamic_update_slice(placed, part.astype(F32)[:, None], (0, core, 0))
            return placed.reshape(part.shape[0], width)

        ups = got["g_up"].reshape(5, width, half)
        up = jnp.concatenate([spread(ups[chunk]) for chunk in range(4)], axis=1)
        start = (freq // 2) * 384 + (freq % 2) * 128
        part_qk, g_qk, g_v = (got["g_qkv%d" % part].reshape(width, -1).astype(F32) for part in range(3))
        own_part = (jnp.arange(128) < 64) == (core == 0)
        parts = jnp.where(own_part, part_qk, 0.0), jnp.where(own_part, jnp.roll(part_qk, 64, 1), 0.0)
        windows = [
            jnp.where(core == 0, jnp.concatenate([whole, part], 1), jnp.concatenate([part, whole], 1))
            for whole, part in zip((g_qk[:, :128], g_qk[:, 128:]), parts)
        ]
        qkv = jnp.concatenate(
            [lax.dynamic_update_slice(jnp.zeros((width, width), F32), part, (0, start)) for part in (*windows, g_v)], axis=1
        )
        mats = scatter(qkv), scatter(spread(ups[4])), scatter(up), scatter(spread(got["g_down"].reshape(4 * width, half)))
        vectors = [scatter(got["vec"][row]) for row in range(8)]
        up_bias_grad = scatter(got["vec"][8:12].reshape(-1))
    qkv_grad, proj_grad, up_grad, down_grad = mats
    gain_one, shift_one, query, value, proj, gain_two, shift_two, down = vectors
    return (
        block_out, grad_tok, gain_one, shift_one, qkv_grad, query, value, proj_grad, proj,
        gain_two, shift_two, up_grad, up_bias_grad, down_grad, down,
    )


def solution(mesh):
    acts, both = P("clip", "freq", None), ("clip", "freq")
    mat, vec = P(both, None), P(both)
    return jax.shard_map(
        on_device,
        mesh=mesh,
        in_specs=(acts, acts, P("clip", None), P("clip")) + (P(),) * 13,
        out_specs=(acts, acts, vec, vec, mat, vec, vec, mat, vec, vec, vec, mat, vec, mat, vec),
        check_vma=False,
    )
```
